256 devices in a mesh: seq: 32 (over x, z), tp: 4 (over y), grp: 2 (over core).
Axes of the slice: x: 4, y: 4, z: 8, core: 2. Of those that a mesh axis runs over, the one named last changes fastest.
Arguments:
- queries: bfloat16 [16384, 4096], P(('seq', 'grp'), 'tp'), may hold values from -40 to 40
- out_grad: bfloat16 [16384, 4096], P(('seq', 'grp'), 'tp'), may hold values from -6 to 6
- query_gain: float32 [128], replicated, may hold values from 0.1 to 1.9
- key_gain: float32 [128], replicated, may hold values from 0.1 to 1.9
- key_weight: bfloat16 [1024, 4096], P(None, 'tp'), may hold values from -1 to 1
- value_weight: bfloat16 [1024, 4096], P(None, 'tp'), may hold values from -0.1875 to 0.1875
- neighbours: bfloat16 [128, 2048, 1024], P(('tp', 'grp'), 'seq'), may hold values from -30 to 30
- neighbour_owner: int32 [256, 2], P(('seq', 'grp')), may hold values from 0 to 31, as said below
- owner_slots: int32 [2048], P('seq'), may hold values from -1 to 511, as said below
Outputs:
- query_grad: bfloat16 [16384, 4096], P(('seq', 'grp'), 'tp')
- neighbour_grad: bfloat16 [128, 2048, 1024], P(('tp', 'grp'), 'seq')
The draws below stay inside these ranges and needn't reach their ends.
Inputs may be any that keep to these rules, and one draw needn't show every extreme that they name: `neighbour_owner`: entry [u, k] is the owner, an index along seq, that holds the k-th neighbour of stretch u. Among the 8 neighbours of the stretches of one index of seq and grp, no owner appears more than 1 times, and in every draw one owner appears exactly 1 times for every such index. `owner_slots`: entries o * 64 to o * 64 + 63 are the slots of owner o; each holds a neighbour number u * 2 + k or -1 where it is empty. Every neighbour is held by exactly one slot of the owner that neighbour_owner names, and one owner's slots are all full in every draw.
All inputs are finite; a program needn't handle non-finite values.
Results may differ from the reference program's by a relative error of at most 0.015.
Values may be sent and summed in bfloat16 or wider, within the bound.
A program may use at most 128 MiB of HBM per device.

```python
import math
import jax
import jax.numpy as jnp
from jax import lax

HEADS = 32
HD = 128
DE = 1024
NR = 128
CH = 64
NB = 2
TOK_DEV = 256
NPD = 8
PCAP = 1
CAP = 64
SLOTS = 2048
TOKENS = 16384
STRETCHES = 256
HW = 4096
N_SEQ = 32
N_GRP = 2


def neighbour_layout(key):
    busiest = jax.random.randint(jax.random.fold_in(key, 101), (), 0, N_SEQ)
    copies = jnp.arange(N_SEQ * PCAP, dtype=jnp.int32) // PCAP

    def one_device(device_key):
        shuffle_key, assign_key = jax.random.split(device_key)
        shuffled = jax.random.permutation(shuffle_key, copies)
        arranged = jnp.argsort((shuffled != busiest).astype(jnp.int32), stable=True)
        chosen = shuffled[arranged][:NPD]
        return jax.random.permutation(assign_key, chosen)
    device_keys = jax.random.split(jax.random.fold_in(key, 102), N_SEQ * N_GRP)
    owners = jax.vmap(one_device)(device_keys).reshape(-1).astype(jnp.int32)
    onehot = (owners[:, None] == jnp.arange(N_SEQ, dtype=jnp.int32)[None, :]).astype(jnp.int32)
    standing = jnp.sum((jnp.cumsum(onehot, axis=0) - onehot) * onehot, axis=1)
    table_keys = jax.random.split(jax.random.fold_in(key, 103), N_SEQ)
    tables = jax.vmap(lambda table_key: jax.random.permutation(table_key, CAP))(table_keys).astype(jnp.int32)
    slot_index = tables[owners, standing]
    position = owners * CAP + slot_index
    slot_lists = jnp.full((N_SEQ * CAP,), -1, jnp.int32).at[position].set(jnp.arange(owners.shape[0], dtype=jnp.int32))
    return (owners.reshape(STRETCHES, NB), slot_lists)


def draw_neighbour_owner(key, part):
    owners, slot_lists = neighbour_layout(key)
    return owners


def draw_owner_slots(key, part):
    owners, slot_lists = neighbour_layout(key)
    return slot_lists


def log_scales(scale_key, shape, lowest, highest):
    return jnp.exp(jax.random.uniform(scale_key, shape, jnp.float32, math.log(lowest), math.log(highest)))


def draw_queries(key, part):
    key = jax.random.fold_in(key, 1)
    noise_key, row_key, col_key = jax.random.split(key, 3)
    base_draw = jax.random.normal(noise_key, (TOKENS, HW), jnp.float32)
    row_scale = log_scales(row_key, (TOKENS, 1), 0.3, 3.0)
    col_scale = log_scales(col_key, (1, HW), 0.3, 3.0)
    return jnp.clip(base_draw * row_scale * col_scale, -40.0, 40.0).astype(jnp.bfloat16)


def draw_neighbours(key, part):
    key = jax.random.fold_in(key, 2)
    noise_key, row_key = jax.random.split(key, 2)
    base_draw = jax.random.normal(noise_key, (NR, SLOTS, DE), jnp.float32)
    row_scale = log_scales(row_key, (NR, SLOTS, 1), 0.3, 3.0)
    return jnp.clip(base_draw * row_scale, -30.0, 30.0).astype(jnp.bfloat16)


def draw_key_weight(key, part):
    key = jax.random.fold_in(key, 3)
    noise_key, col_key = jax.random.split(key, 2)
    base_draw = jax.random.normal(noise_key, (DE, HW), jnp.float32)
    col_scale = log_scales(col_key, (1, HW), 0.3, 3.0)
    return jnp.clip(base_draw * col_scale / math.sqrt(DE), -1.0, 1.0).astype(jnp.bfloat16)


def shard_levels(rng, extent, pieces, low, largest):
    factor_of = 1.0
    for dim, parts in pieces:
        draws = jax.random.uniform(jax.random.fold_in(jax.random.fold_in(rng, 6), dim), (parts,), jnp.float32, low / len(pieces), largest / len(pieces))
        factor_of = factor_of * jnp.repeat(jnp.exp(draws), extent[dim] // parts).reshape((-1,) + (1,) * (len(extent) - 1 - dim))
    return factor_of


def centred(stream_key, extent, deviation, reach, cuts=(), held_as=jnp.bfloat16):
    result = deviation * jax.random.normal(stream_key, extent, jnp.float32)
    if cuts:
        result = result * shard_levels(stream_key, extent, cuts, -0.22, 0.18)
    return jnp.clip(result, -reach, reach).astype(held_as)


def setup_inputs(seed: int = 0) -> dict:
    arg_keys = jax.random.split(jax.random.key(seed), 10)
    return {
        "queries": draw_queries(jax.random.fold_in(arg_keys[9], 71), 0),
        "out_grad": centred(arg_keys[1], (TOKENS, HW), 1.0, 6.0, ((0, 64), (1, 4))),
        "query_gain": jnp.clip(1.0 + 0.18 * jax.random.normal(arg_keys[2], (HD,), jnp.float32), 0.1, 1.9),
        "key_gain": jnp.clip(1.0 + 0.18 * jax.random.normal(arg_keys[3], (HD,), jnp.float32), 0.1, 1.9),
        "key_weight": draw_key_weight(jax.random.fold_in(arg_keys[9], 71), 0),
        "value_weight": centred(arg_keys[5], (DE, HW), DE ** -0.5, 0.1875, ((1, 4),)),
        "neighbours": draw_neighbours(jax.random.fold_in(arg_keys[9], 71), 0),
        "neighbour_owner": draw_neighbour_owner(jax.random.fold_in(arg_keys[9], 71), 0),
        "owner_slots": draw_owner_slots(jax.random.fold_in(arg_keys[9], 71), 0),
    }


EPS = 1e-06

def scale_rows(entries, gain_vector):
    inverse = lax.rsqrt(lax.optimization_barrier(jnp.mean(entries * entries, axis=-1, keepdims=True)) + EPS)
    return entries * inverse * gain_vector

def scale_back(entries, gain_vector, upstream):
    inverse = lax.rsqrt(lax.optimization_barrier(jnp.mean(entries * entries, axis=-1, keepdims=True)) + EPS)
    scaled = upstream * gain_vector
    inner = lax.optimization_barrier(jnp.mean(entries * scaled, axis=-1, keepdims=True))
    return inverse * scaled - entries * (inverse * inverse * inverse) * inner

def reference(queries, out_grad, query_gain, key_gain, key_weight, value_weight, neighbours, neighbour_owner, owner_slots):
    stretches_dev = TOK_DEV // CH
    per_dev = stretches_dev * NB
    block_count = TOKENS // TOK_DEV
    slot_table = owner_slots.reshape(N_SEQ, CAP)
    score_scale = 1.0 / math.sqrt(HD)
    cap_order = jnp.arange(CAP, dtype=jnp.int32)

    def one_block(block_index):
        first_row = block_index * TOK_DEV
        query_block = lax.dynamic_slice_in_dim(queries, first_row, TOK_DEV, 0)
        grad_block = lax.dynamic_slice_in_dim(out_grad, first_row, TOK_DEV, 0)
        owners = lax.dynamic_slice_in_dim(neighbour_owner, block_index * stretches_dev, stretches_dev, 0).reshape(-1)
        neighbour_ids = block_index * per_dev + jnp.arange(per_dev, dtype=jnp.int32)
        slot_lists = slot_table[owners]
        matches = slot_lists == neighbour_ids[:, None]
        within = lax.optimization_barrier(jnp.sum(jnp.where(matches, cap_order[None, :], 0), axis=1)).astype(jnp.int32)
        present = jnp.any(matches, axis=1)
        position = (owners * CAP + within).astype(jnp.int32)
        neighbour_rows = jnp.take(neighbours, position, axis=1) * present[None, :, None].astype(jnp.bfloat16)
        flattened = neighbour_rows.reshape(NR * per_dev, DE)
        raw_keys = jnp.dot(flattened, key_weight, preferred_element_type=jnp.float32).reshape(NR, stretches_dev, NB, HEADS, HD)
        value_rows = jnp.dot(flattened, value_weight, preferred_element_type=jnp.float32).astype(jnp.bfloat16).reshape(NR, stretches_dev, NB, HEADS, HD)
        key_rows = scale_rows(raw_keys, key_gain).astype(jnp.bfloat16)
        query_raw = query_block.astype(jnp.float32).reshape(stretches_dev, CH, HEADS, HD)
        query_norm = scale_rows(query_raw, query_gain).astype(jnp.bfloat16)
        grad_out = grad_block.reshape(stretches_dev, CH, HEADS, HD)
        scores = jnp.einsum('cihd,rckhd->chikr', query_norm.astype(jnp.float32), key_rows.astype(jnp.float32)) * score_scale
        weights = jnp.exp(scores)
        probability = weights / lax.optimization_barrier(jnp.sum(weights, axis=(3, 4), keepdims=True))
        prob_grad = jnp.einsum('cihd,rckhd->chikr', grad_out.astype(jnp.float32), value_rows.astype(jnp.float32))
        inner_sum = lax.optimization_barrier(jnp.sum(probability * prob_grad, axis=(3, 4), keepdims=True))
        score_grad = (probability * (prob_grad - inner_sum)).astype(jnp.bfloat16)
        prob_low = probability.astype(jnp.bfloat16)
        value_grad = jnp.einsum('chikr,cihd->rckhd', prob_low.astype(jnp.float32), grad_out.astype(jnp.float32)).astype(jnp.bfloat16)
        key_back = jnp.einsum('chikr,cihd->rckhd', score_grad.astype(jnp.float32), query_norm.astype(jnp.float32)) * score_scale
        query_back = jnp.einsum('chikr,rckhd->cihd', score_grad.astype(jnp.float32), key_rows.astype(jnp.float32)) * score_scale
        query_grad = scale_back(query_raw, query_gain, query_back).astype(jnp.bfloat16).reshape(TOK_DEV, HW)
        raw_grad = scale_back(raw_keys, key_gain, key_back).astype(jnp.bfloat16).reshape(NR * per_dev, HW)
        value_flat = value_grad.reshape(NR * per_dev, HW)
        contract = (((1,), (1,)), ((), ()))
        encoded_grad = lax.dot_general(raw_grad, key_weight, contract, preferred_element_type=jnp.float32)
        encoded_grad = encoded_grad + lax.dot_general(value_flat, value_weight, contract, preferred_element_type=jnp.float32)
        return (query_grad, encoded_grad.astype(jnp.bfloat16).reshape(NR, per_dev, DE))
    query_grads, block_grads = lax.map(one_block, jnp.arange(block_count, dtype=jnp.int32))
    query_grad = query_grads.reshape(TOKENS, HW)
    all_grads = jnp.moveaxis(block_grads, 1, 0).reshape(NR, block_count * per_dev, DE)
    occupied = owner_slots >= 0
    neighbour_grad = jnp.take(all_grads, jnp.maximum(owner_slots, 0).astype(jnp.int32), axis=1)
    neighbour_grad = neighbour_grad * occupied[None, :, None].astype(jnp.bfloat16)
    return (query_grad, neighbour_grad)
```

```python
import math

import jax
import jax.numpy as jnp
from jax import lax
from jax.experimental import pallas as pl
from jax.experimental.pallas import tpu as pltpu
from jax.sharding import PartitionSpec as P

HD = 128
CH = 64
NB = 2


EPS = 1e-06
SCALE = 1.0 / math.sqrt(HD)
NT = (((1,), (1,)), ((), ()))
TN = (((0,), (0,)), ((), ()))
NN = (((1,), (0,)), ((), ()))


def dot(a, b, dims):
    return lax.dot_general(a, b, dims, preferred_element_type=jnp.float32)


def attend(e_ref, wk_ref, wv_ref, q_ref, go_ref, qg_ref, kg_ref, qgrad_ref, dkr_ref, dv_ref):
    rows, width = q_ref.shape
    stretches = rows // CH
    groups, per_dev, sub, enc = e_ref.shape
    keys = groups * 2 * sub
    qgain = qg_ref[...]
    kgain = kg_ref[...]

    def pair(i, carry):
        cols = pl.ds(pl.multiple_of(i * 2 * HD, 2 * HD), 2 * HD)
        enc_rows = e_ref[...].reshape(groups * per_dev * sub, enc)
        kr2 = dot(enc_rows, wk_ref[:, cols], NN)
        val2 = dot(enc_rows, wv_ref[:, cols], NN).astype(jnp.bfloat16)
        for hh in range(2):
            lanes = slice(hh * HD, (hh + 1) * HD)
            head = pl.ds(pl.multiple_of((i * 2 + hh) * HD, HD), HD)
            kr = kr2[:, lanes]
            val = val2[:, lanes].reshape(groups, per_dev, sub, HD)
            kinv = lax.rsqrt(jnp.mean(kr * kr, axis=-1, keepdims=True) + EPS)
            khat = kr * kinv
            kn = (khat * kgain).astype(jnp.bfloat16).reshape(groups, per_dev, sub, HD)
            khat = khat.reshape(groups, per_dev, sub, HD)
            kinv = kinv.reshape(groups, per_dev, sub, 1)
            qx = q_ref[:, head].astype(jnp.float32)
            qinv = lax.rsqrt(jnp.mean(qx * qx, axis=-1, keepdims=True) + EPS)
            qhat = qx * qinv
            qn = (qhat * qgain).astype(jnp.bfloat16)
            go = go_ref[:, head]
            for c in range(stretches):
                tok = slice(c * CH, (c + 1) * CH)
                kn_c = kn[:, 2 * c:2 * c + 2].reshape(keys, HD)
                val_c = val[:, 2 * c:2 * c + 2].reshape(keys, HD)
                qn_c, go_c = qn[tok], go[tok]
                weights = jnp.exp(dot(qn_c, kn_c, NT) * SCALE)
                prob = weights * (1.0 / jnp.sum(weights, axis=-1, keepdims=True))
                dp = dot(go_c, val_c, NT)
                inner = jnp.sum(prob * dp, axis=-1, keepdims=True)
                ds = (prob * (dp - inner)).astype(jnp.bfloat16)
                pb = prob.astype(jnp.bfloat16)
                dv_c = dot(pb, go_c, TN).astype(jnp.bfloat16)
                dkn = dot(ds, qn_c, TN)
                dqn = dot(ds, kn_c, NN)
                qs = dqn * (qgain * SCALE)
                qh = qhat[tok]
                qi = jnp.mean(qh * qs, axis=-1, keepdims=True)
                qgrad_ref[tok, head] = (qinv[tok] * (qs - qh * qi)).astype(jnp.bfloat16)
                ks = dkn * (kgain * SCALE)
                kh = khat[:, 2 * c:2 * c + 2].reshape(keys, HD)
                ki = jnp.mean(kh * ks, axis=-1, keepdims=True)
                kv = kinv[:, 2 * c:2 * c + 2].reshape(keys, 1)
                dk = (kv * (ks - kh * ki)).astype(jnp.bfloat16)
                dkr_ref[:, 2 * c:2 * c + 2, :, head] = dk.reshape(groups, 2, sub, HD)
                dv_ref[:, 2 * c:2 * c + 2, :, head] = dv_c.reshape(groups, 2, sub, HD)
        return carry
    lax.fori_loop(0, width // (2 * HD), pair, 0)


def compute_kernel(e_ref, wk_ref, wv_ref, q_ref, go_ref, qg_ref, kg_ref, qgrad_ref, de_ref, dkr_ref, dv_ref):
    attend(e_ref, wk_ref, wv_ref, q_ref, go_ref, qg_ref, kg_ref, qgrad_ref, dkr_ref, dv_ref)
    groups, per_dev, sub, enc = e_ref.shape
    width = q_ref.shape[1]

    def back(j, carry):
        cols = pl.ds(pl.multiple_of(j * 256, 256), 256)
        total = dot(dkr_ref[...].reshape(-1, width), wk_ref[cols, :], NT)
        total = total + dot(dv_ref[...].reshape(-1, width), wv_ref[cols, :], NT)
        de_ref[:, :, :, cols] = total.astype(jnp.bfloat16).reshape(groups, per_dev, sub, 256)
        return carry
    lax.fori_loop(0, enc // 256, back, 0)


def compute(e, wk, wv, q, go, qg, kg):
    vm = pl.BlockSpec(memory_space=pltpu.VMEM)
    return pl.pallas_call(
        compute_kernel,
        out_shape=(jax.ShapeDtypeStruct(q.shape, jnp.bfloat16), jax.ShapeDtypeStruct(e.shape, jnp.bfloat16)),
        in_specs=[vm] * 7,
        out_specs=(vm, vm),
        scratch_shapes=[pltpu.VMEM(e.shape, jnp.bfloat16), pltpu.VMEM(e.shape, jnp.bfloat16)],
        name="attention",
        compiler_params=pltpu.CompilerParams(vmem_limit_bytes=56 * 2**20),
    )(e, wk, wv, q, go, qg.reshape(1, HD), kg.reshape(1, HD))


def shards(
    queries,
    out_grad,
    query_gain,
    key_gain,
    key_weight,
    value_weight,
    neighbours,
    neighbour_owner,
    owner_slots,
):
    tok_rows, col_width = queries.shape
    stretches_dev = tok_rows // CH
    per_dev = stretches_dev * NB
    seq_count = lax.axis_size("seq")
    grp_count = lax.axis_size("grp")
    slot_count = owner_slots.shape[0]
    pair_cap = slot_count // (grp_count * seq_count)
    slot_span = seq_count * pair_cap
    rows_own = neighbours.shape[0]
    rows_tp = rows_own * grp_count
    enc_width = neighbours.shape[2]
    occupied = owner_slots >= 0
    target_dev = jnp.where(occupied, owner_slots // NB // stretches_dev, -1)
    dest_seq = target_dev // grp_count
    dest_grp = target_dev % grp_count
    slot_order = jnp.arange(slot_count, dtype=jnp.int32)
    same_dest = (target_dev[:, None] == target_dev[None, :]) & (
        owner_slots[None, :] < owner_slots[:, None]
    )
    pair_rank = jnp.sum(same_dest.astype(jnp.int32), axis=1)
    target = jnp.where(occupied, dest_grp * slot_span + dest_seq * pair_cap + pair_rank, -1)
    chooser = (
        (slot_order[:, None] == target[None, :])
        .astype(jnp.bfloat16)
        .reshape(grp_count, slot_span, slot_count)
    )
    outgoing = jnp.einsum(
        "gqs,rsd->rgqd", chooser, neighbours, preferred_element_type=jnp.float32
    ).astype(jnp.bfloat16)
    arrived = lax.all_to_all(
        lax.all_to_all(outgoing, "seq", split_axis=2, concat_axis=2, tiled=True),
        "grp",
        split_axis=1,
        concat_axis=0,
        tiled=True,
    )
    arrived = arrived.reshape(rows_tp, slot_span, enc_width)
    owners = neighbour_owner.reshape(-1)
    positions = jnp.arange(per_dev, dtype=jnp.int32)
    earlier = (owners[:, None] == owners[None, :]) & (positions[None, :] < positions[:, None])
    picked = owners * pair_cap + jnp.sum(earlier.astype(jnp.int32), axis=1)
    used_rows = jnp.take(arrived, picked, axis=1)
    shard_piece = lax.all_gather(used_rows, "tp", axis=0, tiled=True)
    groups = shard_piece.shape[0] // 16
    enc = shard_piece.reshape(groups, 16, per_dev, enc_width).transpose(0, 2, 1, 3)
    query_grad, enc_grad = compute(
        enc, key_weight, value_weight, queries, out_grad, query_gain, key_gain
    )
    term_rows = enc_grad.transpose(0, 2, 1, 3)
    summed = lax.psum_scatter(
        term_rows.reshape(lax.axis_size("tp") * rows_tp, per_dev, enc_width),
        "tp",
        scatter_dimension=0,
        tiled=True,
    )
    outbound = jnp.zeros((rows_tp, slot_span, enc_width), jnp.bfloat16).at[:, picked].set(summed)
    outbound = outbound.reshape(rows_tp, 1, slot_span, enc_width)
    returned = lax.all_to_all(
        lax.all_to_all(outbound, "seq", split_axis=2, concat_axis=2, tiled=True),
        "grp",
        split_axis=0,
        concat_axis=1,
        tiled=True,
    )
    neighbour_grad = jnp.einsum(
        "gqs,rgqd->rsd", chooser, returned, preferred_element_type=jnp.float32
    ).astype(jnp.bfloat16)
    return (query_grad, neighbour_grad)


def solution(mesh):
    in_specs = (
        P(("seq", "grp"), "tp"),
        P(("seq", "grp"), "tp"),
        P(),
        P(),
        P(None, "tp"),
        P(None, "tp"),
        P(("tp", "grp"), "seq", None),
        P(("seq", "grp"), None),
        P("seq"),
    )
    out_specs = (P(("seq", "grp"), "tp"), P(("tp", "grp"), "seq", None))
    return jax.shard_map(shards, mesh=mesh, in_specs=in_specs, out_specs=out_specs, check_vma=False)
```

```python
import functools
import math

import jax
import jax.numpy as jnp
from jax import lax
from jax.experimental import pallas as pl
from jax.experimental.pallas import tpu as pltpu
from jax.sharding import PartitionSpec as P

HD = 128
CH = 64
EPS = 1e-06
SCALE = 1.0 / math.sqrt(HD)
NT = (((1,), (1,)), ((), ()))
TN = (((0,), (0,)), ((), ()))
NN = (((1,), (0,)), ((), ()))


def dot(a, b, dims):
    return lax.dot_general(a, b, dims, preferred_element_type=jnp.float32)


def attend(e_ref, wk_ref, wv_ref, q_ref, go_ref, qg_ref, kg_ref, qgrad_ref, dkr_ref, dv_ref):
    rows, width = q_ref.shape
    stretches = rows // CH
    groups, per_dev, sub, enc = e_ref.shape
    keys = groups * 2 * sub
    qgain = qg_ref[...]
    kgain = kg_ref[...]

    def pair(i, carry):
        cols = pl.ds(pl.multiple_of(i * 2 * HD, 2 * HD), 2 * HD)
        enc_rows = e_ref[...].reshape(groups * per_dev * sub, enc)
        kr2 = dot(enc_rows, wk_ref[:, cols], NN)
        val2 = dot(enc_rows, wv_ref[:, cols], NN).astype(jnp.bfloat16)
        for hh in range(2):
            lanes = slice(hh * HD, (hh + 1) * HD)
            head = pl.ds(pl.multiple_of((i * 2 + hh) * HD, HD), HD)
            kr = kr2[:, lanes]
            val = val2[:, lanes].reshape(groups, per_dev, sub, HD)
            kinv = lax.rsqrt(jnp.mean(kr * kr, axis=-1, keepdims=True) + EPS)
            khat = kr * kinv
            kn = (khat * kgain).astype(jnp.bfloat16).reshape(groups, per_dev, sub, HD)
            khat = khat.reshape(groups, per_dev, sub, HD)
            kinv = kinv.reshape(groups, per_dev, sub, 1)
            qx = q_ref[:, head].astype(jnp.float32)
            qinv = lax.rsqrt(jnp.mean(qx * qx, axis=-1, keepdims=True) + EPS)
            qhat = qx * qinv
            qn = (qhat * qgain).astype(jnp.bfloat16)
            go = go_ref[:, head]
            for c in range(stretches):
                tok = slice(c * CH, (c + 1) * CH)
                kn_c = kn[:, 2 * c:2 * c + 2].reshape(keys, HD)
                val_c = val[:, 2 * c:2 * c + 2].reshape(keys, HD)
                qn_c, go_c = qn[tok], go[tok]
                weights = jnp.exp(dot(qn_c, kn_c, NT) * SCALE)
                prob = weights * (1.0 / jnp.sum(weights, axis=-1, keepdims=True))
                dp = dot(go_c, val_c, NT)
                inner = jnp.sum(prob * dp, axis=-1, keepdims=True)
                ds = (prob * (dp - inner)).astype(jnp.bfloat16)
                pb = prob.astype(jnp.bfloat16)
                dv_c = dot(pb, go_c, TN).astype(jnp.bfloat16)
                dkn = dot(ds, qn_c, TN)
                dqn = dot(ds, kn_c, NN)
                qs = dqn * (qgain * SCALE)
                qh = qhat[tok]
                qi = jnp.mean(qh * qs, axis=-1, keepdims=True)
                qgrad_ref[tok, head] = (qinv[tok] * (qs - qh * qi)).astype(jnp.bfloat16)
                ks = dkn * (kgain * SCALE)
                kh = khat[:, 2 * c:2 * c + 2].reshape(keys, HD)
                ki = jnp.mean(kh * ks, axis=-1, keepdims=True)
                kv = kinv[:, 2 * c:2 * c + 2].reshape(keys, 1)
                dk = (kv * (ks - kh * ki)).astype(jnp.bfloat16)
                dkr_ref[:, 2 * c:2 * c + 2, :, head] = dk.reshape(groups, 2, sub, HD)
                dv_ref[:, 2 * c:2 * c + 2, :, head] = dv_c.reshape(groups, 2, sub, HD)
        return carry
    lax.fori_loop(0, width // (2 * HD), pair, 0)


def compute_kernel(e_ref, wk_ref, wv_ref, q_ref, go_ref, qg_ref, kg_ref, qgrad_ref, de_ref, dkr_ref, dv_ref):
    attend(e_ref, wk_ref, wv_ref, q_ref, go_ref, qg_ref, kg_ref, qgrad_ref, dkr_ref, dv_ref)
    groups, per_dev, sub, enc = e_ref.shape
    width = q_ref.shape[1]

    def back(j, carry):
        cols = pl.ds(pl.multiple_of(j * 256, 256), 256)
        total = dot(dkr_ref[...].reshape(-1, width), wk_ref[cols, :], NT)
        total = total + dot(dv_ref[...].reshape(-1, width), wv_ref[cols, :], NT)
        de_ref[:, :, :, cols] = total.astype(jnp.bfloat16).reshape(groups, per_dev, sub, 256)
        return carry
    lax.fori_loop(0, enc // 256, back, 0)


def compute(e, wk, wv, q, go, qg, kg):
    vm = pl.BlockSpec(memory_space=pltpu.VMEM)
    return pl.pallas_call(
        compute_kernel,
        out_shape=(jax.ShapeDtypeStruct(q.shape, jnp.bfloat16), jax.ShapeDtypeStruct(e.shape, jnp.bfloat16)),
        in_specs=[vm] * 7,
        out_specs=(vm, vm),
        scratch_shapes=[pltpu.VMEM(e.shape, jnp.bfloat16), pltpu.VMEM(e.shape, jnp.bfloat16)],
        name="attention",
        compiler_params=pltpu.CompilerParams(vmem_limit_bytes=56 * 2**20),
    )(e, wk, wv, q, go, qg.reshape(1, HD), kg.reshape(1, HD))


MESH = pl.DeviceIdType.MESH
NX, NZ, NT_DEV, NG = 4, 8, 4, 2
SUB = 16
PER = 8


def place():
    s = lax.axis_index("seq")
    return s // NZ, s % NZ, lax.axis_index("tp"), lax.axis_index("grp")


def at(x, z, t, g):
    return (lax.rem(x + NX, NX) * NZ + lax.rem(z + NZ, NZ), lax.rem(t + NT_DEV, NT_DEV), lax.rem(g + NG, NG))


X_PEERS = [(k, 0, 0, 0) for k in (1, 2, 3)]
Z_PEERS = [(0, k, 0, 0) for k in (1, -1, 2, -2, 3, -3)]
Y_PEERS = [(0, 0, t, g) for t in range(NT_DEV) for g in range(NG) if (t, g) != (0, 0)]
META_PEERS = [(0, 1, 0, 1), (0, -1, 0, 1)]


def greet(peers):
    x, z, t, g = place()
    barrier = pltpu.get_barrier_semaphore()
    for dx, dz, dt, dg in peers:
        pl.semaphore_signal(barrier, inc=1, device_id=at(x + dx, z + dz, t + dt, g + dg), device_id_type=MESH)


def met(peers):
    pl.semaphore_wait(pltpu.get_barrier_semaphore(), len(peers))


def push(src, dst, send, recv, device):
    pltpu.make_async_remote_copy(
        src_ref=src, dst_ref=dst, send_sem=send, recv_sem=recv, device_id=device, device_id_type=MESH
    ).start()


def arrive(view, sem):
    pltpu.make_async_copy(view, view, sem).wait()


def choose(tiles, picks, index):
    result = tiles[0]
    for k in range(1, len(tiles)):
        result = jnp.where(index == picks[k], tiles[k], result)
    return result


def dispatch_kernel(
    chunks, t_ref, no_ref, nb_ref, e_ref, meta_ref,
    perm, sent, xr, zb, mg, zr, fin, meta, mets,
    x_s, x_r, z1_s, z1_r, z2_s, z2_r, y_s, y_r, m_s, m_r, m_l,
):
    x, z, t, g = place()
    wide = nb_ref.shape[2] // chunks
    peers = X_PEERS + Z_PEERS + Y_PEERS + META_PEERS
    greet(peers)

    lane = lax.broadcasted_iota(jnp.int32, (8, 128), 1)
    row = jnp.zeros((8, 128), jnp.int32)
    for p in range(PER):
        owner = no_ref[0, p]
        row = jnp.where(lane == p, owner, row)
        row = jnp.where(lane == PER + owner, p, row)
    meta[1 * NG + g] = row
    size = t_ref.shape[1]
    order = lax.broadcasted_iota(jnp.int32, (size, size), 0)
    perm[...] = (order == t_ref[...]).astype(jnp.bfloat16)
    met(peers)
    mine = meta.at[NG + g]
    push(mine, mine, m_s, m_r, at(x, z, t, g + 1))
    for dg in range(NG):
        push(mine, meta.at[g], m_s, m_r, at(x, z + 1, t, g + dg))
        push(mine, meta.at[2 * NG + g], m_s, m_r, at(x, z - 1, t, g + dg))

    def columns(c):
        return pl.ds(pl.multiple_of(c * wide, wide), wide)

    def stage_x(c):
        rows = nb_ref[:, :, columns(c)].reshape(size, wide)
        sent[c] = dot(perm[...], rows, NN).astype(jnp.bfloat16).reshape(NX, NZ, NG, SUB, wide)
        for dx, _, _, _ in X_PEERS:
            to = lax.rem(x + dx, NX)
            push(sent.at[c, to], xr.at[c, :, :, x], x_s.at[c], x_r.at[c], at(to, z, t, g))
        pltpu.make_async_copy(sent.at[c, x], xr.at[c, :, :, x], x_r.at[c]).start()

    def stage_z1(c):
        arrive(xr.at[c], x_r.at[c])
        for way, sign in ((0, 1), (1, -1)):
            for k in (3, 2, 1):
                dest = lax.rem(z + sign * (k + 1) + NZ, NZ)
                if k == 3:
                    src, dst = xr.at[c, dest, way], zb.at[c, way, 4]
                else:
                    src, dst = xr.at[c, dest], zb.at[c, way, pl.ds(2 * (k - 1), 2)]
                push(src, dst, z1_s.at[c], z1_r.at[c], at(x, z + sign * k, t, g))

    def stage_z2(c):
        arrive(zb.at[c], z1_r.at[c])
        for way, sign in ((0, 1), (1, -1)):
            dest = lax.rem(z + sign + NZ, NZ)
            for h in range(NG):
                far = 3 if h == way else 2
                tiles = [xr[c, dest, h, xo] for xo in range(NX)]
                for k in range(1, far + 1):
                    part = 4 if k == 3 else 2 * (k - 1) + h
                    tiles += [zb[c, way, part, xo] for xo in range(NX)]
                for p in range(PER):
                    owner = mets[(1 + sign) * NG + h, 0, p]
                    rel = lax.rem(sign * (z - lax.rem(owner, NZ)) + NZ, NZ)
                    mg[c, way, h, p] = choose(tiles, range(len(tiles)), rel * NX + owner // NZ)
            push(mg.at[c, way], zr.at[c, way], z2_s.at[c], z2_r.at[c], at(x, z + sign, t, g))

    def stage_y(c):
        arrive(mg.at[c], z2_r.at[c])
        for h in range(NG):
            own = [xr[c, z, h, xo] for xo in range(NX)]
            for p in range(PER):
                owner = mets[NG + h, 0, p]
                rel = lax.rem(z - lax.rem(owner, NZ) + NZ, NZ)
                back = jnp.where(rel >= (5 if h == 0 else 4), zr[c, 1, h, p], zr[c, 0, h, p])
                near = choose(own, range(NX), owner // NZ)
                fin[c, h, p] = jnp.where(rel == 0, near, back)
        slot = t * NG + g
        for _, _, dt, dg in Y_PEERS:
            to = lax.rem(g + dg, NG)
            push(fin.at[c, to], e_ref.at[slot, :, :, columns(c)], y_s.at[c], y_r.at[c], at(x, z, t + dt, to))
        pltpu.make_async_copy(fin.at[c, g], e_ref.at[slot, :, :, columns(c)], y_r.at[c]).start()

    def step(i, carry):
        @pl.when(i < chunks)
        def _():
            stage_x(i)

        @pl.when((i >= 1) & (i <= chunks))
        def _():
            stage_z1(i - 1)

        @pl.when(i == 1)
        def _():
            arrive(meta.at[pl.ds(0, 5)], m_r)
            copy = pltpu.make_async_copy(meta, mets, m_l)
            copy.start()
            copy.wait()

        @pl.when((i >= 2) & (i <= chunks + 1))
        def _():
            stage_z2(i - 2)

        @pl.when(i >= 3)
        def _():
            stage_y(i - 3)
        return carry
    lax.fori_loop(0, chunks + 3, step, 0)

    def drain(c, carry):
        arrive(e_ref.at[:, :, :, columns(c)], y_r.at[c])
        arrive(sent.at[c, pl.ds(0, 3)], x_s.at[c])
        arrive(zb.at[c], z1_s.at[c])
        arrive(mg.at[c], z2_s.at[c])
        arrive(e_ref.at[pl.ds(0, 7), :, :, columns(c)], y_s.at[c])
        return carry
    lax.fori_loop(0, chunks, drain, 0)
    arrive(meta.at[pl.ds(0, 5)], m_s)
    meta_ref[...] = meta[...]


def dispatch(chunks, t_row, owners, neighbours):
    sub, slots, enc = neighbours.shape
    wide = enc // chunks
    vm = pl.BlockSpec(memory_space=pltpu.VMEM)
    tile = (SUB, wide)
    bf = jnp.bfloat16
    dma = pltpu.SemaphoreType.DMA
    return pl.pallas_call(
        functools.partial(dispatch_kernel, chunks),
        out_shape=(
            jax.ShapeDtypeStruct((NT_DEV * NG, PER, SUB, enc), bf),
            jax.ShapeDtypeStruct((3 * NG, 8, 128), jnp.int32),
        ),
        in_specs=[vm, pl.BlockSpec(memory_space=pltpu.SMEM), vm],
        out_specs=(vm, vm),
        scratch_shapes=[
            pltpu.VMEM((sub * slots, sub * slots), bf),
            pltpu.VMEM((chunks, NX, NZ, NG) + tile, bf),
            pltpu.VMEM((chunks, NZ, NG, NX) + tile, bf),
            pltpu.VMEM((chunks, 2, 5, NX) + tile, bf),
            pltpu.VMEM((chunks, 2, NG, PER) + tile, bf),
            pltpu.VMEM((chunks, 2, NG, PER) + tile, bf),
            pltpu.VMEM((chunks, NG, PER) + tile, bf),
            pltpu.VMEM((3 * NG, 8, 128), jnp.int32),
            pltpu.SMEM((3 * NG, 8, 128), jnp.int32),
        ] + [dma((chunks,))] * 8 + [dma, dma, dma],
        name="dispatch",
        compiler_params=pltpu.CompilerParams(
            collective_id=0, has_side_effects=True, vmem_limit_bytes=56 * 2**20
        ),
    )(t_row, owners, neighbours)


def return_kernel(
    chunks, t_ref, mets, d_ref, out_ref,
    perm, yr, gs, r1, fw, rz, fr,
    y_s, y_r, r1_s, r1_r, r2_s, r2_r, x_s, x_r,
):
    x, z, t, g = place()
    wide = out_ref.shape[2] // chunks
    peers = X_PEERS + Z_PEERS + Y_PEERS
    greet(peers)
    size = t_ref.shape[0]
    order = lax.broadcasted_iota(jnp.int32, (size, size), 1)
    perm[...] = (order == t_ref[...]).astype(jnp.bfloat16)
    met(peers)

    def columns(c):
        return pl.ds(pl.multiple_of(c * wide, wide), wide)

    def stage_y(c):
        slot = t * NG + g
        for _, _, dt, dg in Y_PEERS:
            tt, gg = lax.rem(t + dt, NT_DEV), lax.rem(g + dg, NG)
            push(d_ref.at[tt * NG + gg, :, :, columns(c)], yr.at[c, slot], y_s.at[c], y_r.at[c], at(x, z, tt, gg))
        pltpu.make_async_copy(d_ref.at[slot, :, :, columns(c)], yr.at[c, slot], y_r.at[c]).start()

    def stage_r1(c):
        arrive(yr.at[c], y_r.at[c])
        for h in range(NG):
            total = yr[c, h].astype(jnp.float32)
            for k in range(1, NT_DEV):
                total = total + yr[c, k * NG + h].astype(jnp.float32)
            gs[c, h] = total.astype(jnp.bfloat16)
        push(gs.at[c], r1.at[c, 0], r1_s.at[c], r1_r.at[c], at(x, z + 1, t, g))
        push(gs.at[c], r1.at[c, 1], r1_s.at[c], r1_r.at[c], at(x, z - 1, t, g))

    def select(tiles, near, h, row, xo):
        position = mets[near * NG + h, 0, PER + xo * NZ + row]
        return choose(tiles, range(PER), position)

    def stage_r2(c):
        arrive(r1.at[c], r1_r.at[c])
        for way, sign in ((0, 1), (1, -1)):
            near = 0 if way == 0 else 2
            block = lax.rem(z - sign + NZ, NZ)
            for h in range(NG):
                far = 3 if h == way else 2
                tiles = [r1[c, way, h, p] for p in range(PER)]
                for k in range(far + 1):
                    row = lax.rem(z + sign * k + NZ, NZ)
                    part = 4 if k == 3 else 2 * (k - 1) + h
                    for xo in range(NX):
                        value = select(tiles, near, h, row, xo)
                        if k == 0:
                            rz[c, block, h, xo] = value
                        else:
                            fw[c, way, part, xo] = value
            for k in (3, 2, 1):
                if k == 3:
                    src, dst = fw.at[c, way, 4], rz.at[c, block, way]
                else:
                    src, dst = fw.at[c, way, pl.ds(2 * (k - 1), 2)], rz.at[c, block]
                push(src, dst, r2_s.at[c], r2_r.at[c], at(x, z + sign * k, t, g))
        for h in range(NG):
            tiles = [gs[c, h, p] for p in range(PER)]
            for xo in range(NX):
                rz[c, z, h, xo] = select(tiles, 1, h, z, xo)

    def stage_x(c):
        arrive(fw.at[c], r2_r.at[c])
        for dx, _, _, _ in X_PEERS:
            to = lax.rem(x + dx, NX)
            push(rz.at[c, :, :, to], fr.at[c, x], x_s.at[c], x_r.at[c], at(to, z, t, g))
        pltpu.make_async_copy(rz.at[c, :, :, x], fr.at[c, x], x_r.at[c]).start()

    def stage_out(c):
        arrive(fr.at[c], x_r.at[c])
        rows = fr[c].reshape(size, wide)
        placed = dot(perm[...], rows, NN).astype(jnp.bfloat16)
        out_ref[:, :, columns(c)] = placed.reshape(out_ref.shape[0], out_ref.shape[1], wide)

    def step(i, carry):
        for k, stage in enumerate((stage_y, stage_r1, stage_r2, stage_x, stage_out)):
            @pl.when((i >= k) & (i < chunks + k))
            def _(stage=stage, k=k):
                stage(i - k)
        return carry
    lax.fori_loop(0, chunks + 4, step, 0)

    def drain(c, carry):
        arrive(d_ref.at[pl.ds(0, 7), :, :, columns(c)], y_s.at[c])
        arrive(r1.at[c], r1_s.at[c])
        arrive(fw.at[c], r2_s.at[c])
        arrive(fr.at[c, pl.ds(0, 3)], x_s.at[c])
        return carry
    lax.fori_loop(0, chunks, drain, 0)


def give_back(chunks, t_col, mets, partial, slots):
    groups, per, sub, enc = partial.shape
    wide = enc // chunks
    vm = pl.BlockSpec(memory_space=pltpu.VMEM)
    tile = (SUB, wide)
    bf = jnp.bfloat16
    dma = pltpu.SemaphoreType.DMA
    return pl.pallas_call(
        functools.partial(return_kernel, chunks),
        out_shape=jax.ShapeDtypeStruct((sub, slots, enc), bf),
        in_specs=[vm, pl.BlockSpec(memory_space=pltpu.SMEM), vm],
        out_specs=vm,
        scratch_shapes=[
            pltpu.VMEM((sub * slots, sub * slots), bf),
            pltpu.VMEM((chunks, NT_DEV * NG, PER) + tile, bf),
            pltpu.VMEM((chunks, NG, PER) + tile, bf),
            pltpu.VMEM((chunks, 2, NG, PER) + tile, bf),
            pltpu.VMEM((chunks, 2, 5, NX) + tile, bf),
            pltpu.VMEM((chunks, NZ, NG, NX) + tile, bf),
            pltpu.VMEM((chunks, NX, NZ, NG) + tile, bf),
        ] + [dma((chunks,))] * 8,
        name="give_back",
        compiler_params=pltpu.CompilerParams(
            collective_id=1, has_side_effects=True, vmem_limit_bytes=56 * 2**20
        ),
    )(t_col, mets, partial)


def targets(owner_slots):
    block = jnp.where(owner_slots >= 0, owner_slots // PER, -SUB) * SUB
    return (block[None, :] + jnp.arange(SUB, dtype=jnp.int32)[:, None]).reshape(-1)


CHUNKS = 8


def shards(
    queries,
    out_grad,
    query_gain,
    key_gain,
    key_weight,
    value_weight,
    neighbours,
    neighbour_owner,
    owner_slots,
):
    target = targets(owner_slots)
    enc, meta = dispatch(CHUNKS, target.reshape(1, -1), neighbour_owner.reshape(1, -1), neighbours)
    query_grad, partial = compute(
        enc, key_weight, value_weight, queries, out_grad, query_gain, key_gain
    )
    neighbour_grad = give_back(CHUNKS, target.reshape(-1, 1), meta, partial, owner_slots.shape[0])
    return (query_grad, neighbour_grad)


def solution(mesh):
    in_specs = (
        P(("seq", "grp"), "tp"),
        P(("seq", "grp"), "tp"),
        P(),
        P(),
        P(None, "tp"),
        P(None, "tp"),
        P(("tp", "grp"), "seq", None),
        P(("seq", "grp"), None),
        P("seq"),
    )
    out_specs = (P(("seq", "grp"), "tp"), P(("tp", "grp"), "seq", None))
    return jax.shard_map(shards, mesh=mesh, in_specs=in_specs, out_specs=out_specs, check_vma=False)
```

```python
import functools
import math

import jax
import jax.numpy as jnp
from jax import lax
from jax.experimental import pallas as pl
from jax.experimental.pallas import tpu as pltpu
from jax.sharding import PartitionSpec as P

HD = 128
CH = 64
EPS = 1e-06
SCALE = 1.0 / math.sqrt(HD)
NT = (((1,), (1,)), ((), ()))
TN = (((0,), (0,)), ((), ()))
NN = (((1,), (0,)), ((), ()))
MESH = pl.DeviceIdType.MESH
NX, NZ, NT_DEV, NG = 4, 8, 4, 2
SUB = 16
PER = 8
CHUNKS = 8


def dot(a, b, dims):
    return lax.dot_general(a, b, dims, preferred_element_type=jnp.float32)


def place():
    s = lax.axis_index("seq")
    return s // NZ, s % NZ, lax.axis_index("tp"), lax.axis_index("grp")


def at(x, z, t, g):
    return (lax.rem(x + NX, NX) * NZ + lax.rem(z + NZ, NZ), lax.rem(t + NT_DEV, NT_DEV), lax.rem(g + NG, NG))


X_PEERS = [(k, 0, 0, 0) for k in (1, 2, 3)]
Z_PEERS = [(0, k, 0, 0) for k in (1, -1, 2, -2, 3, -3)]
Y_PEERS = [(0, 0, t, g) for t in range(NT_DEV) for g in range(NG) if (t, g) != (0, 0)]
META_PEERS = [(0, 1, 0, 1), (0, -1, 0, 1)]


def greet(peers):
    x, z, t, g = place()
    barrier = pltpu.get_barrier_semaphore()
    for dx, dz, dt, dg in peers:
        pl.semaphore_signal(barrier, inc=1, device_id=at(x + dx, z + dz, t + dt, g + dg), device_id_type=MESH)


def met(peers):
    pl.semaphore_wait(pltpu.get_barrier_semaphore(), len(peers))


def push(src, dst, send, recv, device):
    pltpu.make_async_remote_copy(
        src_ref=src, dst_ref=dst, send_sem=send, recv_sem=recv, device_id=device, device_id_type=MESH
    ).start()


def arrive(view, sem):
    pltpu.make_async_copy(view, view, sem).wait()


def choose(tiles, picks, index):
    result = tiles[0]
    for k in range(1, len(tiles)):
        result = jnp.where(index == picks[k], tiles[k], result)
    return result


def attend(e_ref, kacc, vacc, wk_ref, wv_ref, q_ref, go_ref, qg_ref, kg_ref, qgrad_ref, dkr_ref, dv_ref):
    rows, width = q_ref.shape
    stretches = rows // CH
    groups, per_dev, sub, enc = e_ref.shape
    keys = groups * 2 * sub
    qgain = qg_ref[...]
    kgain = kg_ref[...]

    def pair(i, carry):
        cols = pl.ds(pl.multiple_of(i * 2 * HD, 2 * HD), 2 * HD)
        last = slice(enc - 256, enc)
        enc_rows = e_ref[:, :, :, last].reshape(groups * per_dev * sub, 256)
        kr2 = kacc[:, cols] + dot(enc_rows, wk_ref[last, cols], NN)
        val2 = (vacc[:, cols] + dot(enc_rows, wv_ref[last, cols], NN)).astype(jnp.bfloat16)
        for hh in range(2):
            lanes = slice(hh * HD, (hh + 1) * HD)
            head = pl.ds(pl.multiple_of((i * 2 + hh) * HD, HD), HD)
            kr = kr2[:, lanes]
            val = val2[:, lanes].reshape(groups, per_dev, sub, HD)
            kinv = lax.rsqrt(jnp.mean(kr * kr, axis=-1, keepdims=True) + EPS)
            khat = kr * kinv
            kn = (khat * kgain).astype(jnp.bfloat16).reshape(groups, per_dev, sub, HD)
            khat = khat.reshape(groups, per_dev, sub, HD)
            kinv = kinv.reshape(groups, per_dev, sub, 1)
            qx = q_ref[:, head].astype(jnp.float32)
            qinv = lax.rsqrt(jnp.mean(qx * qx, axis=-1, keepdims=True) + EPS)
            qhat = qx * qinv
            qn = (qhat * qgain).astype(jnp.bfloat16)
            go = go_ref[:, head]
            for c in range(stretches):
                tok = slice(c * CH, (c + 1) * CH)
                kn_c = kn[:, 2 * c:2 * c + 2].reshape(keys, HD)
                val_c = val[:, 2 * c:2 * c + 2].reshape(keys, HD)
                qn_c, go_c = qn[tok], go[tok]
                weights = jnp.exp(dot(qn_c, kn_c, NT) * SCALE)
                prob = weights * (1.0 / jnp.sum(weights, axis=-1, keepdims=True))
                dp = dot(go_c, val_c, NT)
                inner = jnp.sum(prob * dp, axis=-1, keepdims=True)
                ds = (prob * (dp - inner)).astype(jnp.bfloat16)
                pb = prob.astype(jnp.bfloat16)
                dv_c = dot(pb, go_c, TN).astype(jnp.bfloat16)
                dkn = dot(ds, qn_c, TN)
                dqn = dot(ds, kn_c, NN)
                qs = dqn * (qgain * SCALE)
                qh = qhat[tok]
                qi = jnp.mean(qh * qs, axis=-1, keepdims=True)
                qgrad_ref[tok, head] = (qinv[tok] * (qs - qh * qi)).astype(jnp.bfloat16)
                ks = dkn * (kgain * SCALE)
                kh = khat[:, 2 * c:2 * c + 2].reshape(keys, HD)
                ki = jnp.mean(kh * ks, axis=-1, keepdims=True)
                kv = kinv[:, 2 * c:2 * c + 2].reshape(keys, 1)
                dk = (kv * (ks - kh * ki)).astype(jnp.bfloat16)
                dkr_ref[:, 2 * c:2 * c + 2, :, head] = dk.reshape(groups, 2, sub, HD)
                dv_ref[:, 2 * c:2 * c + 2, :, head] = dv_c.reshape(groups, 2, sub, HD)
        return carry
    lax.fori_loop(0, width // (2 * HD), pair, 0)


def kernel(
    slots_ref, no_ref, qg_ref, kg_ref, nb_hbm, wk_hbm, wv_hbm, q_hbm, go_hbm,
    qgrad_hbm, out_hbm,
    nb, wk, wv, q, go, qgrad, perm, perm_back,
    sent, xr, zb, mg, zr, fin, enc, kacc, vacc, dkr, dv,
    part, yr, gs, r1, fw, rz, fr, placed_ref, meta, mets,
    x_s, x_r, z1_s, z1_r, z2_s, z2_r, y_s, y_r,
    by_s, by_r, r1_s, r1_r, r2_s, r2_r, bx_s, bx_r, out_sem,
    m_s, m_r, m_l, in_sem, q_sem,
):
    x, z, t, g = place()
    chunks = CHUNKS
    wide = nb.shape[2] // chunks
    slots = nb.shape[1]
    size = SUB * slots
    peers = X_PEERS + Z_PEERS + Y_PEERS + META_PEERS
    greet(peers)
    loads = [
        pltpu.make_async_copy(src, dst, in_sem.at[k])
        for k, (src, dst) in enumerate(((nb_hbm, nb), (wk_hbm, wk), (wv_hbm, wv), (q_hbm, q), (go_hbm, go)))
    ]
    for load in loads:
        load.start()

    lane8 = lax.broadcasted_iota(jnp.int32, (8, 128), 1)
    row = jnp.zeros((8, 128), jnp.int32)
    for p in range(PER):
        owner = no_ref[p // 2, p % 2]
        row = jnp.where(lane8 == p, owner, row)
        row = jnp.where(lane8 == PER + owner, p, row)
    meta[1 * NG + g] = row

    def block(s):
        number = slots_ref[s]
        return jnp.where(number >= 0, number // PER, -SUB) * SUB

    lane = lax.broadcasted_iota(jnp.int32, (1, 128), 1)
    base = jnp.zeros((1, 128), jnp.int32)
    for s in range(slots):
        base = jnp.where(lax.rem(lane, slots) == s, block(s), base)
    base = base + lane // slots
    order = lax.broadcasted_iota(jnp.int32, (size, 128), 0)
    for k in range(size // 128):
        perm[:, k * 128:(k + 1) * 128] = (order == base + k * (128 // slots)).astype(jnp.bfloat16)
    met(peers)
    mine = meta.at[NG + g]
    push(mine, mine, m_s, m_r, at(x, z, t, g + 1))
    for dg in range(NG):
        push(mine, meta.at[g], m_s, m_r, at(x, z + 1, t, g + dg))
        push(mine, meta.at[2 * NG + g], m_s, m_r, at(x, z - 1, t, g + dg))
    loads[0].wait()

    def columns(c):
        return pl.ds(pl.multiple_of(c * wide, wide), wide)

    def stage_x(c):
        rows = nb[:, :, columns(c)].reshape(size, wide)
        sent[c] = dot(perm[...], rows, NN).astype(jnp.bfloat16).reshape(NX, NZ, NG, SUB, wide)
        for dx, _, _, _ in X_PEERS:
            to = lax.rem(x + dx, NX)
            push(sent.at[c, to], xr.at[c, :, :, x], x_s.at[c], x_r.at[c], at(to, z, t, g))
        pltpu.make_async_copy(sent.at[c, x], xr.at[c, :, :, x], x_r.at[c]).start()

    def stage_z1(c):
        arrive(xr.at[c], x_r.at[c])
        for way, sign in ((0, 1), (1, -1)):
            for k in (3, 2, 1):
                dest = lax.rem(z + sign * (k + 1) + NZ, NZ)
                if k == 3:
                    src, dst = xr.at[c, dest, way], zb.at[c, way, 4]
                else:
                    src, dst = xr.at[c, dest], zb.at[c, way, pl.ds(2 * (k - 1), 2)]
                push(src, dst, z1_s.at[c], z1_r.at[c], at(x, z + sign * k, t, g))

    def stage_z2(c):
        arrive(zb.at[c], z1_r.at[c])
        for way, sign in ((0, 1), (1, -1)):
            dest = lax.rem(z + sign + NZ, NZ)
            for h in range(NG):
                far = 3 if h == way else 2
                tiles = [xr[c, dest, h, xo] for xo in range(NX)]
                for k in range(1, far + 1):
                    part = 4 if k == 3 else 2 * (k - 1) + h
                    tiles += [zb[c, way, part, xo] for xo in range(NX)]
                for p in range(PER):
                    owner = mets[(1 + sign) * NG + h, 0, p]
                    rel = lax.rem(sign * (z - lax.rem(owner, NZ)) + NZ, NZ)
                    mg[c, way, h, p] = choose(tiles, range(len(tiles)), rel * NX + owner // NZ)
            push(mg.at[c, way], zr.at[c, way], z2_s.at[c], z2_r.at[c], at(x, z + sign, t, g))

    def stage_y(c):
        arrive(mg.at[c], z2_r.at[c])
        for h in range(NG):
            own = [xr[c, z, h, xo] for xo in range(NX)]
            for p in range(PER):
                owner = mets[NG + h, 0, p]
                rel = lax.rem(z - lax.rem(owner, NZ) + NZ, NZ)
                back = jnp.where(rel >= (5 if h == 0 else 4), zr[c, 1, h, p], zr[c, 0, h, p])
                near = choose(own, range(NX), owner // NZ)
                fin[c, h, p] = jnp.where(rel == 0, near, back)
        slot = t * NG + g
        for _, _, dt, dg in Y_PEERS:
            to = lax.rem(g + dg, NG)
            push(fin.at[c, to], enc.at[slot, :, :, columns(c)], y_s.at[c], y_r.at[c], at(x, z, t + dt, to))
        pltpu.make_async_copy(fin.at[c, g], enc.at[slot, :, :, columns(c)], y_r.at[c]).start()

    def project(j):
        rows = pl.ds(pl.multiple_of(j * 256, 256), 256)
        left = enc[:, :, :, rows].reshape(size, 256)

        def block_of(k, carry):
            cols = pl.ds(pl.multiple_of(k * 256, 256), 256)
            for acc, weight in ((kacc, wk), (vacc, wv)):
                term = dot(left, weight[rows, cols], NN)

                @pl.when(j == 0)
                def _(acc=acc, term=term):
                    acc[:, cols] = term

                @pl.when(j > 0)
                def _(acc=acc, term=term):
                    acc[:, cols] += term
            return carry
        lax.fori_loop(0, wk.shape[1] // 256, block_of, 0)

    def stage_p(c):
        arrive(enc.at[:, :, :, columns(c)], y_r.at[c])

        @pl.when(c == 0)
        def _():
            for load in loads[1:]:
                load.wait()

        @pl.when((lax.rem(c, 2) == 1) & (c < chunks - 1))
        def _():
            project(c // 2)

    def step(i, carry):
        @pl.when(i < chunks)
        def _():
            stage_x(i)

        @pl.when((i >= 1) & (i <= chunks))
        def _():
            stage_z1(i - 1)

        @pl.when(i == 1)
        def _():
            arrive(meta.at[pl.ds(0, 5)], m_r)
            copy = pltpu.make_async_copy(meta, mets, m_l)
            copy.start()
            copy.wait()

        @pl.when((i >= 2) & (i <= chunks + 1))
        def _():
            stage_z2(i - 2)

        @pl.when((i >= 3) & (i <= chunks + 2))
        def _():
            stage_y(i - 3)

        @pl.when(i >= 4)
        def _():
            stage_p(i - 4)
        return carry
    lax.fori_loop(0, chunks + 4, step, 0)

    attend(enc, kacc, vacc, wk, wv, q, go, qg_ref, kg_ref, qgrad, dkr, dv)
    give = pltpu.make_async_copy(qgrad, qgrad_hbm, q_sem)
    give.start()

    def back_y(c):
        slot = t * NG + g
        rows = columns(c)
        total = dot(dkr[...].reshape(size, -1), wk[rows, :], NT)
        total = total + dot(dv[...].reshape(size, -1), wv[rows, :], NT)
        part[c] = total.astype(jnp.bfloat16).reshape(NT_DEV * NG, PER, SUB, wide)
        for _, _, dt, dg in Y_PEERS:
            tt, gg = lax.rem(t + dt, NT_DEV), lax.rem(g + dg, NG)
            push(part.at[c, tt * NG + gg], yr.at[c, slot], by_s.at[c], by_r.at[c], at(x, z, tt, gg))
        pltpu.make_async_copy(part.at[c, slot], yr.at[c, slot], by_r.at[c]).start()

    def back_r1(c):
        arrive(yr.at[c], by_r.at[c])
        for h in range(NG):
            total = yr[c, h].astype(jnp.float32)
            for k in range(1, NT_DEV):
                total = total + yr[c, k * NG + h].astype(jnp.float32)
            gs[c, h] = total.astype(jnp.bfloat16)
        push(gs.at[c], r1.at[c, 0], r1_s.at[c], r1_r.at[c], at(x, z + 1, t, g))
        push(gs.at[c], r1.at[c, 1], r1_s.at[c], r1_r.at[c], at(x, z - 1, t, g))

    def select(tiles, near, h, row, xo):
        position = mets[near * NG + h, 0, PER + xo * NZ + row]
        return choose(tiles, range(PER), position)

    def back_r2(c):
        arrive(r1.at[c], r1_r.at[c])
        for way, sign in ((0, 1), (1, -1)):
            near = 0 if way == 0 else 2
            block = lax.rem(z - sign + NZ, NZ)
            for h in range(NG):
                far = 3 if h == way else 2
                tiles = [r1[c, way, h, p] for p in range(PER)]
                for k in range(far + 1):
                    row = lax.rem(z + sign * k + NZ, NZ)
                    part = 4 if k == 3 else 2 * (k - 1) + h
                    for xo in range(NX):
                        value = select(tiles, near, h, row, xo)
                        if k == 0:
                            rz[c, block, h, xo] = value
                        else:
                            fw[c, way, part, xo] = value
            for k in (3, 2, 1):
                if k == 3:
                    src, dst = fw.at[c, way, 4], rz.at[c, block, way]
                else:
                    src, dst = fw.at[c, way, pl.ds(2 * (k - 1), 2)], rz.at[c, block]
                push(src, dst, r2_s.at[c], r2_r.at[c], at(x, z + sign * k, t, g))
        for h in range(NG):
            tiles = [gs[c, h, p] for p in range(PER)]
            for xo in range(NX):
                rz[c, z, h, xo] = select(tiles, 1, h, z, xo)

    def back_x(c):
        arrive(fw.at[c], r2_r.at[c])
        for dx, _, _, _ in X_PEERS:
            to = lax.rem(x + dx, NX)
            push(rz.at[c, :, :, to], fr.at[c, x], bx_s.at[c], bx_r.at[c], at(to, z, t, g))
        pltpu.make_async_copy(rz.at[c, :, :, x], fr.at[c, x], bx_r.at[c]).start()

    def back_out(c):
        arrive(fr.at[c], bx_r.at[c])
        rows = fr[c].reshape(size, wide)
        placed = dot(perm_back[...], rows, NN).astype(jnp.bfloat16)
        placed_ref[c] = placed.reshape(SUB, slots, wide)
        pltpu.make_async_copy(placed_ref.at[c], out_hbm.at[:, :, columns(c)], out_sem.at[c]).start()

    def back_step(i, carry):
        for k, stage in enumerate((back_y, back_r1, back_r2, back_x, back_out)):
            @pl.when((i >= k) & (i < chunks + k))
            def _(stage=stage, k=k):
                stage(i - k)

        @pl.when(i == 0)
        def _():
            order = lax.broadcasted_iota(jnp.int32, (size, 128), 1)
            down = lax.broadcasted_iota(jnp.int32, (8, 128), 0)
            parts = []
            for k in range(slots // 8):
                value = jnp.zeros((8, 128), jnp.int32)
                for s in range(8):
                    value = jnp.where(down == s, block(k * 8 + s), value)
                parts.append(value)
            rows = jnp.concatenate(parts, axis=0)
            rows = jnp.concatenate([rows + r for r in range(SUB)], axis=0)
            for k in range(size // 128):
                perm_back[:, k * 128:(k + 1) * 128] = (order + k * 128 == rows).astype(jnp.bfloat16)
        return carry
    lax.fori_loop(0, chunks + 4, back_step, 0)

    def drain(c, carry):
        arrive(sent.at[c, pl.ds(0, 3)], x_s.at[c])
        arrive(zb.at[c], z1_s.at[c])
        arrive(mg.at[c], z2_s.at[c])
        arrive(part.at[c, pl.ds(0, 7)], y_s.at[c])
        arrive(part.at[c, pl.ds(0, 7)], by_s.at[c])
        arrive(r1.at[c], r1_s.at[c])
        arrive(fw.at[c], r2_s.at[c])
        arrive(fr.at[c, pl.ds(0, 3)], bx_s.at[c])
        pltpu.make_async_copy(placed_ref.at[c], out_hbm.at[:, :, columns(c)], out_sem.at[c]).wait()
        return carry
    lax.fori_loop(0, chunks, drain, 0)
    arrive(meta.at[pl.ds(0, 5)], m_s)
    give.wait()


def shards(
    queries,
    out_grad,
    query_gain,
    key_gain,
    key_weight,
    value_weight,
    neighbours,
    neighbour_owner,
    owner_slots,
):
    tokens, width = queries.shape
    sub, slots, deep = neighbours.shape
    bf = jnp.bfloat16
    f32 = jnp.float32
    size = sub * slots
    end = (SUB, deep // CHUNKS)
    rows = (NT_DEV * NG, PER, SUB, deep)
    vm = pl.BlockSpec(memory_space=pltpu.VMEM)
    sm = pl.BlockSpec(memory_space=pltpu.SMEM)
    hbm = pl.BlockSpec(memory_space=pl.ANY)
    dma = pltpu.SemaphoreType.DMA

    def tiles(*lead):
        return pltpu.VMEM((CHUNKS,) + lead + end, bf)
    scratch = [
        pltpu.VMEM(neighbours.shape, bf),
        pltpu.VMEM(key_weight.shape, bf),
        pltpu.VMEM(value_weight.shape, bf),
        pltpu.VMEM(queries.shape, bf),
        pltpu.VMEM(out_grad.shape, bf),
        pltpu.VMEM(queries.shape, bf),
        pltpu.VMEM((size, size), bf),
        pltpu.VMEM((size, size), bf),
        tiles(NX, NZ, NG),
        tiles(NZ, NG, NX),
        tiles(2, 5, NX),
        tiles(2, NG, PER),
        tiles(2, NG, PER),
        tiles(NG, PER),
        pltpu.VMEM(rows, bf),
        pltpu.VMEM((size, width), f32),
        pltpu.VMEM((size, width), f32),
        pltpu.VMEM(rows[:3] + (width,), bf),
        pltpu.VMEM(rows[:3] + (width,), bf),
        tiles(NT_DEV * NG, PER),
        tiles(NT_DEV * NG, PER),
        tiles(NG, PER),
        tiles(2, NG, PER),
        tiles(2, 5, NX),
        tiles(NZ, NG, NX),
        tiles(NX, NZ, NG),
        pltpu.VMEM((CHUNKS, sub, slots, deep // CHUNKS), bf),
        pltpu.VMEM((3 * NG, 8, 128), jnp.int32),
        pltpu.SMEM((3 * NG, 8, 128), jnp.int32),
    ]
    scratch += [dma((CHUNKS,))] * 17 + [dma, dma, dma, dma((5,)), dma]
    return pl.pallas_call(
        kernel,
        out_shape=(
            jax.ShapeDtypeStruct(queries.shape, bf),
            jax.ShapeDtypeStruct(neighbours.shape, bf),
        ),
        in_specs=[sm, sm, vm, vm] + [hbm] * 5,
        out_specs=(hbm, hbm),
        scratch_shapes=scratch,
        name="cross_attention_back",
        compiler_params=pltpu.CompilerParams(
            collective_id=0, has_side_effects=True, vmem_limit_bytes=60 * 2**20
        ),
    )(
        owner_slots, neighbour_owner, query_gain.reshape(1, HD), key_gain.reshape(1, HD),
        neighbours, key_weight, value_weight, queries, out_grad,
    )


def solution(mesh):
    in_specs = (
        P(("seq", "grp"), "tp"),
        P(("seq", "grp"), "tp"),
        P(),
        P(),
        P(None, "tp"),
        P(None, "tp"),
        P(("tp", "grp"), "seq", None),
        P(("seq", "grp"), None),
        P("seq"),
    )
    out_specs = (P(("seq", "grp"), "tp"), P(("tp", "grp"), "seq", None))
    return jax.shard_map(shards, mesh=mesh, in_specs=in_specs, out_specs=out_specs, check_vma=False)
```

```python
import functools
import math

import jax
import jax.numpy as jnp
from jax import lax
from jax.experimental import pallas as pl
from jax.experimental.pallas import tpu as pltpu
from jax.sharding import PartitionSpec as P

HD = 128
CH = 64
EPS = 1e-06
SCALE = 1.0 / math.sqrt(HD)
NT = (((1,), (1,)), ((), ()))
TN = (((0,), (0,)), ((), ()))
NN = (((1,), (0,)), ((), ()))
MESH = pl.DeviceIdType.MESH
NX, NZ, NT_DEV, NG = 4, 8, 4, 2
SUB = 16
PER = 8
CHUNKS = 8


def dot(a, b, dims):
    return lax.dot_general(a, b, dims, preferred_element_type=jnp.float32)


def place():
    s = lax.axis_index("seq")
    return s // NZ, s % NZ, lax.axis_index("tp"), lax.axis_index("grp")


def at(x, z, t, g):
    return (lax.rem(x + NX, NX) * NZ + lax.rem(z + NZ, NZ), lax.rem(t + NT_DEV, NT_DEV), lax.rem(g + NG, NG))


X_PEERS = [(k, 0, 0, 0) for k in (1, 2, 3)]
Z_PEERS = [(0, k, 0, 0) for k in (1, -1, 2, -2, 3, -3)]
Y_PEERS = [(0, 0, t, g) for t in range(NT_DEV) for g in range(NG) if (t, g) != (0, 0)]
META_PEERS = [(0, 1, 0, 1), (0, -1, 0, 1)]


def greet(peers):
    x, z, t, g = place()
    barrier = pltpu.get_barrier_semaphore()
    for dx, dz, dt, dg in peers:
        pl.semaphore_signal(barrier, inc=1, device_id=at(x + dx, z + dz, t + dt, g + dg), device_id_type=MESH)


def met(peers):
    pl.semaphore_wait(pltpu.get_barrier_semaphore(), len(peers))


def push(src, dst, send, recv, device):
    pltpu.make_async_remote_copy(
        src_ref=src, dst_ref=dst, send_sem=send, recv_sem=recv, device_id=device, device_id_type=MESH
    ).start()


def arrive(view, sem):
    pltpu.make_async_copy(view, view, sem).wait()


def choose(tiles, picks, index):
    result = tiles[0]
    for k in range(1, len(tiles)):
        result = jnp.where(index == picks[k], tiles[k], result)
    return result


def attend(e_ref, kacc, vacc, wk_ref, wv_ref, q_ref, go_ref, qg_ref, kg_ref, qgrad_ref, dkr_ref, dv_ref):
    rows, width = q_ref.shape
    stretches = rows // CH
    groups, per_dev, sub, enc = e_ref.shape
    keys = groups * 2 * sub
    qgain = qg_ref[...]
    kgain = kg_ref[...]

    def pair(i, carry):
        cols = pl.ds(pl.multiple_of(i * 2 * HD, 2 * HD), 2 * HD)
        last = slice(enc - 256, enc)
        enc_rows = e_ref[:, :, :, last].reshape(groups * per_dev * sub, 256)
        kr2 = kacc[:, cols] + dot(enc_rows, wk_ref[last, cols], NN)
        val2 = (vacc[:, cols] + dot(enc_rows, wv_ref[last, cols], NN)).astype(jnp.bfloat16)
        for hh in range(2):
            lanes = slice(hh * HD, (hh + 1) * HD)
            head = pl.ds(pl.multiple_of((i * 2 + hh) * HD, HD), HD)
            kr = kr2[:, lanes]
            val = val2[:, lanes].reshape(groups, per_dev, sub, HD)
            kinv = lax.rsqrt(jnp.mean(kr * kr, axis=-1, keepdims=True) + EPS)
            khat = kr * kinv
            kn = (khat * kgain).astype(jnp.bfloat16).reshape(groups, per_dev, sub, HD)
            khat = khat.reshape(groups, per_dev, sub, HD)
            kinv = kinv.reshape(groups, per_dev, sub, 1)
            qx = q_ref[:, head].astype(jnp.float32)
            qinv = lax.rsqrt(jnp.mean(qx * qx, axis=-1, keepdims=True) + EPS)
            qhat = qx * qinv
            qn = (qhat * qgain).astype(jnp.bfloat16)
            go = go_ref[:, head]
            for c in range(stretches):
                tok = slice(c * CH, (c + 1) * CH)
                kn_c = kn[:, 2 * c:2 * c + 2].reshape(keys, HD)
                val_c = val[:, 2 * c:2 * c + 2].reshape(keys, HD)
                qn_c, go_c = qn[tok], go[tok]
                weights = jnp.exp(dot(qn_c, kn_c, NT) * SCALE)
                prob = weights * (1.0 / jnp.sum(weights, axis=-1, keepdims=True))
                dp = dot(go_c, val_c, NT)
                inner = jnp.sum(prob * dp, axis=-1, keepdims=True)
                ds = (prob * (dp - inner)).astype(jnp.bfloat16)
                pb = prob.astype(jnp.bfloat16)
                dv_c = dot(pb, go_c, TN).astype(jnp.bfloat16)
                dkn = dot(ds, qn_c, TN)
                dqn = dot(ds, kn_c, NN)
                qs = dqn * (qgain * SCALE)
                qh = qhat[tok]
                qi = jnp.mean(qh * qs, axis=-1, keepdims=True)
                qgrad_ref[tok, head] = (qinv[tok] * (qs - qh * qi)).astype(jnp.bfloat16)
                ks = dkn * (kgain * SCALE)
                kh = khat[:, 2 * c:2 * c + 2].reshape(keys, HD)
                ki = jnp.mean(kh * ks, axis=-1, keepdims=True)
                kv = kinv[:, 2 * c:2 * c + 2].reshape(keys, 1)
                dk = (kv * (ks - kh * ki)).astype(jnp.bfloat16)
                dkr_ref[:, 2 * c:2 * c + 2, :, head] = dk.reshape(groups, 2, sub, HD)
                dv_ref[:, 2 * c:2 * c + 2, :, head] = dv_c.reshape(groups, 2, sub, HD)
        return carry
    lax.fori_loop(0, width // (2 * HD), pair, 0)


def kernel(
    slots_ref, no_ref, qg_ref, kg_ref, nb_hbm, wk_hbm, wv_hbm, q_hbm, go_hbm,
    qgrad_hbm, out_hbm,
    nb, wk, wv, q, go, qgrad, perm, perm_back,
    sent, xr, zb, mg, zr, fin, enc, kacc, vacc, dkr, dv,
    part, yr, gs, r1, fw, rz, fr, placed_ref, meta, mets,
    x_s, x_r, z1_s, z1_r, z2_s, z2_r, y_s, y_r,
    by_s, by_r, r1_s, r1_r, r2_s, r2_r, bx_s, bx_r, out_sem,
    e_s, e_r, m_s, m_r, m_l, in_sem, q_sem,
):
    x, z, t, g = place()
    chunks = CHUNKS
    wide = nb.shape[2] // chunks
    slots = nb.shape[1]
    size = SUB * slots
    peers = X_PEERS + Z_PEERS + Y_PEERS + META_PEERS
    greet(peers)
    loads = [
        pltpu.make_async_copy(src, dst, in_sem.at[k])
        for k, (src, dst) in enumerate(((nb_hbm, nb), (wk_hbm, wk), (wv_hbm, wv), (q_hbm, q), (go_hbm, go)))
    ]
    for load in loads:
        load.start()

    lane8 = lax.broadcasted_iota(jnp.int32, (8, 128), 1)
    row = jnp.zeros((8, 128), jnp.int32)
    for p in range(PER):
        owner = no_ref[p % 2, p // 2]
        row = jnp.where(lane8 == p, owner, row)
        row = jnp.where(lane8 == PER + owner, p, row)
    meta[1 * NG + g] = row

    def block(s):
        number = slots_ref[s]
        return jnp.where(number >= 0, number // PER, -SUB) * SUB

    lane = lax.broadcasted_iota(jnp.int32, (1, 128), 1)
    base = jnp.zeros((1, 128), jnp.int32)
    for s in range(slots):
        base = jnp.where(lax.rem(lane, slots) == s, block(s), base)
    base = base + lane // slots
    order = lax.broadcasted_iota(jnp.int32, (size, 128), 0)
    for k in range(size // 128):
        perm[:, k * 128:(k + 1) * 128] = (order == base + k * (128 // slots)).astype(jnp.bfloat16)
    met(peers)
    mine = meta.at[NG + g]
    push(mine, mine, m_s, m_r, at(x, z, t, g + 1))
    for dg in range(NG):
        push(mine, meta.at[g], m_s, m_r, at(x, z + 1, t, g + dg))
        push(mine, meta.at[2 * NG + g], m_s, m_r, at(x, z - 1, t, g + dg))
    loads[0].wait()

    def columns(c):
        return pl.ds(pl.multiple_of(c * wide, wide), wide)

    def stage_x(j):
        cols = pl.ds(pl.multiple_of(j * 2 * wide, 2 * wide), 2 * wide)
        sorted_rows = dot(perm[...], nb[:, :, cols].reshape(size, 2 * wide), NN).astype(jnp.bfloat16)
        for k in range(2):
            c = 2 * j + k
            half = sorted_rows[:, k * wide:(k + 1) * wide]
            sent[c] = half.reshape(NX, NZ, NG, SUB, wide)
            for dx, _, _, _ in X_PEERS:
                to = lax.rem(x + dx, NX)
                push(sent.at[c, to], xr.at[c, NX - dx], x_s.at[c], x_r.at[c], at(to, z, t, g))
            pltpu.make_async_copy(sent.at[c, x], xr.at[c, 0], x_r.at[c]).start()
        both = pl.ds(2 * j, 2)
        for way, sign in ((0, 1), (1, -1)):
            for k in (3, 2, 1):
                dest = lax.rem(z + sign * (k + 1) + NZ, NZ)
                if k == 3:
                    src, dst = sent.at[both, x, dest, way], zb.at[both, way, 0, 4]
                else:
                    src, dst = sent.at[both, x, dest], zb.at[both, way, 0, pl.ds(2 * (k - 1), 2)]
                push(src, dst, e_s.at[j], e_r.at[j], at(x, z + sign * k, t, g))

    def stage_z1(c):
        arrive(xr.at[c], x_r.at[c])
        others = pl.ds(1, NX - 1)
        for way, sign in ((0, 1), (1, -1)):
            for k in (3, 2, 1):
                dest = lax.rem(z + sign * (k + 1) + NZ, NZ)
                if k == 3:
                    src, dst = xr.at[c, others, dest, way], zb.at[c, way, others, 4]
                else:
                    src, dst = xr.at[c, others, dest], zb.at[c, way, others, pl.ds(2 * (k - 1), 2)]
                push(src, dst, z1_s.at[c], z1_r.at[c], at(x, z + sign * k, t, g))

    def column(owner):
        return lax.rem(owner // NZ - x + NX, NX)

    def stage_z2(c):
        @pl.when(lax.rem(c, 2) == 0)
        def _():
            arrive(zb.at[pl.ds(c, 2), :, 0], e_r.at[c // 2])
        arrive(zb.at[c, :, pl.ds(1, NX - 1)], z1_r.at[c])
        for way, sign in ((0, 1), (1, -1)):
            dest = lax.rem(z + sign + NZ, NZ)
            for h in range(NG):
                far = 3 if h == way else 2
                tiles = [xr[c, k, dest, h] for k in range(NX)]
                for k in range(1, far + 1):
                    part = 4 if k == 3 else 2 * (k - 1) + h
                    tiles += [zb[c, way, j, part] for j in range(NX)]
                for p in range(PER):
                    owner = mets[(1 + sign) * NG + h, 0, p]
                    rel = lax.rem(sign * (z - lax.rem(owner, NZ)) + NZ, NZ)
                    mg[c, way, h, p] = choose(tiles, range(len(tiles)), rel * NX + column(owner))
            push(mg.at[c, way], zr.at[c, way], z2_s.at[c], z2_r.at[c], at(x, z + sign, t, g))

    def stage_y(c):
        arrive(mg.at[c], z2_r.at[c])
        for h in range(NG):
            own = [xr[c, k, z, h] for k in range(NX)]
            for p in range(PER):
                owner = mets[NG + h, 0, p]
                rel = lax.rem(z - lax.rem(owner, NZ) + NZ, NZ)
                back = jnp.where(rel >= (5 if h == 0 else 4), zr[c, 1, h, p], zr[c, 0, h, p])
                near = choose(own, range(NX), column(owner))
                fin[c, h, p] = jnp.where(rel == 0, near, back)
        slot = t * NG + g
        for _, _, dt, dg in Y_PEERS:
            to = lax.rem(g + dg, NG)
            push(fin.at[c, to], enc.at[slot, :, :, columns(c)], y_s.at[c], y_r.at[c], at(x, z, t + dt, to))
        pltpu.make_async_copy(fin.at[c, g], enc.at[slot, :, :, columns(c)], y_r.at[c]).start()

    def project(j):
        rows = pl.ds(pl.multiple_of(j * 256, 256), 256)
        left = enc[:, :, :, rows].reshape(size, 256)

        def block_of(k, carry):
            cols = pl.ds(pl.multiple_of(k * 256, 256), 256)
            for acc, weight in ((kacc, wk), (vacc, wv)):
                term = dot(left, weight[rows, cols], NN)

                @pl.when(j == 0)
                def _(acc=acc, term=term):
                    acc[:, cols] = term

                @pl.when(j > 0)
                def _(acc=acc, term=term):
                    acc[:, cols] += term
            return carry
        lax.fori_loop(0, wk.shape[1] // 256, block_of, 0)

    def stage_p(c):
        arrive(enc.at[:, :, :, columns(c)], y_r.at[c])

        @pl.when(c == 0)
        def _():
            for load in loads[1:]:
                load.wait()

        @pl.when((lax.rem(c, 2) == 1) & (c < chunks - 1))
        def _():
            project(c // 2)

    for j in range(chunks // 2):
        stage_x(j)
    arrive(meta.at[pl.ds(0, 5)], m_r)
    copy = pltpu.make_async_copy(meta, mets, m_l)
    copy.start()
    copy.wait()

    def step(i, carry):
        for lag, stage in ((0, stage_z1), (2, stage_z2), (3, stage_y), (5, stage_p)):
            @pl.when((i >= lag) & (i < chunks + lag))
            def _(stage=stage, lag=lag):
                stage(i - lag)
        return carry
    lax.fori_loop(0, chunks + 5, step, 0)

    attend(enc, kacc, vacc, wk, wv, q, go, qg_ref, kg_ref, qgrad, dkr, dv)
    give = pltpu.make_async_copy(qgrad, qgrad_hbm, q_sem)
    give.start()

    def back_y(c):
        slot = t * NG + g
        rows = columns(c)
        total = dot(dkr[...].reshape(size, -1), wk[rows, :], NT)
        total = total + dot(dv[...].reshape(size, -1), wv[rows, :], NT)
        part[c] = total.astype(jnp.bfloat16).reshape(NT_DEV * NG, PER, SUB, wide)
        for _, _, dt, dg in Y_PEERS:
            tt, gg = lax.rem(t + dt, NT_DEV), lax.rem(g + dg, NG)
            push(part.at[c, tt * NG + gg], yr.at[c, slot], by_s.at[c], by_r.at[c], at(x, z, tt, gg))
        pltpu.make_async_copy(part.at[c, slot], yr.at[c, slot], by_r.at[c]).start()

    def back_r1(c):
        arrive(yr.at[c], by_r.at[c])
        for h in range(NG):
            total = yr[c, h].astype(jnp.float32)
            for k in range(1, NT_DEV):
                total = total + yr[c, k * NG + h].astype(jnp.float32)
            gs[c, h] = total.astype(jnp.bfloat16)
        push(gs.at[c], r1.at[c, 0], r1_s.at[c], r1_r.at[c], at(x, z + 1, t, g))
        push(gs.at[c], r1.at[c, 1], r1_s.at[c], r1_r.at[c], at(x, z - 1, t, g))

    def select(tiles, near, h, row, xo):
        position = mets[near * NG + h, 0, PER + xo * NZ + row]
        return choose(tiles, range(PER), position)

    def back_r2(c):
        arrive(r1.at[c], r1_r.at[c])
        for way, sign in ((0, 1), (1, -1)):
            near = 0 if way == 0 else 2
            block = lax.rem(z - sign + NZ, NZ)
            for h in range(NG):
                far = 3 if h == way else 2
                tiles = [r1[c, way, h, p] for p in range(PER)]
                for k in range(far + 1):
                    row = lax.rem(z + sign * k + NZ, NZ)
                    part = 4 if k == 3 else 2 * (k - 1) + h
                    for xo in range(NX):
                        value = select(tiles, near, h, row, xo)
                        if k == 0:
                            rz[c, block, h, xo] = value
                        else:
                            fw[c, way, part, xo] = value
            for k in (3, 2, 1):
                if k == 3:
                    src, dst = fw.at[c, way, 4], rz.at[c, block, way]
                else:
                    src, dst = fw.at[c, way, pl.ds(2 * (k - 1), 2)], rz.at[c, block]
                push(src, dst, r2_s.at[c], r2_r.at[c], at(x, z + sign * k, t, g))
        for h in range(NG):
            tiles = [gs[c, h, p] for p in range(PER)]
            for xo in range(NX):
                rz[c, z, h, xo] = select(tiles, 1, h, z, xo)

    def back_x(c):
        arrive(fw.at[c], r2_r.at[c])
        for dx, _, _, _ in X_PEERS:
            to = lax.rem(x + dx, NX)
            push(rz.at[c, :, :, to], fr.at[c, x], bx_s.at[c], bx_r.at[c], at(to, z, t, g))
        pltpu.make_async_copy(rz.at[c, :, :, x], fr.at[c, x], bx_r.at[c]).start()

    def back_out(c):
        arrive(fr.at[c], bx_r.at[c])
        rows = fr[c].reshape(size, wide)
        placed = dot(perm_back[...], rows, NN).astype(jnp.bfloat16)
        placed_ref[c] = placed.reshape(SUB, slots, wide)
        pltpu.make_async_copy(placed_ref.at[c], out_hbm.at[:, :, columns(c)], out_sem.at[c]).start()

    def back_step(i, carry):
        for lag, stage in ((4, back_r2), (2, back_r1), (0, back_y), (5, back_x), (6, back_out)):
            @pl.when((i >= lag) & (i < chunks + lag))
            def _(stage=stage, lag=lag):
                stage(i - lag)

        @pl.when(i == 0)
        def _():
            order = lax.broadcasted_iota(jnp.int32, (size, 128), 1)
            down = lax.broadcasted_iota(jnp.int32, (8, 128), 0)
            parts = []
            for k in range(slots // 8):
                value = jnp.zeros((8, 128), jnp.int32)
                for s in range(8):
                    value = jnp.where(down == s, block(k * 8 + s), value)
                parts.append(value)
            rows = jnp.concatenate(parts, axis=0)
            rows = jnp.concatenate([rows + r for r in range(SUB)], axis=0)
            for k in range(size // 128):
                perm_back[:, k * 128:(k + 1) * 128] = (order + k * 128 == rows).astype(jnp.bfloat16)
        return carry
    lax.fori_loop(0, chunks + 6, back_step, 0)

    def drain(c, carry):
        arrive(sent.at[c, pl.ds(0, 3)], x_s.at[c])
        arrive(zb.at[c, :, pl.ds(1, NX - 1)], z1_s.at[c])
        arrive(mg.at[c], z2_s.at[c])
        arrive(part.at[c, pl.ds(0, 7)], y_s.at[c])
        arrive(part.at[c, pl.ds(0, 7)], by_s.at[c])
        arrive(r1.at[c], r1_s.at[c])
        arrive(fw.at[c], r2_s.at[c])
        arrive(fr.at[c, pl.ds(0, 3)], bx_s.at[c])
        pltpu.make_async_copy(placed_ref.at[c], out_hbm.at[:, :, columns(c)], out_sem.at[c]).wait()
        return carry
    lax.fori_loop(0, chunks, drain, 0)
    for j in range(chunks // 2):
        arrive(zb.at[pl.ds(2 * j, 2), :, 0], e_s.at[j])
    arrive(meta.at[pl.ds(0, 5)], m_s)
    give.wait()


def settle_kernel(a_ref, b_ref, x_ref, y_ref):
    x_ref[...] = a_ref[...]
    y_ref[...] = b_ref[...]


def settle(a, b):
    steps = 4
    a_spec = pl.BlockSpec((a.shape[0] // steps, a.shape[1]), lambda i: (i, 0))
    b_spec = pl.BlockSpec((b.shape[0] // steps,) + b.shape[1:], lambda i: (i, 0, 0))
    return pl.pallas_call(
        settle_kernel,
        grid=(steps,),
        out_shape=(jax.ShapeDtypeStruct(a.shape, a.dtype), jax.ShapeDtypeStruct(b.shape, b.dtype)),
        in_specs=[a_spec, b_spec],
        out_specs=(a_spec, b_spec),
        name="settle",
    )(a, b)


def shards(
    queries,
    out_grad,
    query_gain,
    key_gain,
    key_weight,
    value_weight,
    neighbours,
    neighbour_owner,
    owner_slots,
):
    tokens, width = queries.shape
    sub, slots, deep = neighbours.shape
    bf = jnp.bfloat16
    f32 = jnp.float32
    size = sub * slots
    end = (SUB, deep // CHUNKS)
    rows = (NT_DEV * NG, PER, SUB, deep)
    vm = pl.BlockSpec(memory_space=pltpu.VMEM)
    sm = pl.BlockSpec(memory_space=pltpu.SMEM)
    hbm = pl.BlockSpec(memory_space=pl.ANY)
    dma = pltpu.SemaphoreType.DMA

    def tiles(*lead):
        return pltpu.VMEM((CHUNKS,) + lead + end, bf)
    scratch = [
        pltpu.VMEM(neighbours.shape, bf),
        pltpu.VMEM(key_weight.shape, bf),
        pltpu.VMEM(value_weight.shape, bf),
        pltpu.VMEM(queries.shape, bf),
        pltpu.VMEM(out_grad.shape, bf),
        pltpu.VMEM(queries.shape, bf),
        pltpu.VMEM((size, size), bf),
        pltpu.VMEM((size, size), bf),
        tiles(NX, NZ, NG),
        tiles(NX, NZ, NG),
        tiles(2, NX, 5),
        tiles(2, NG, PER),
        tiles(2, NG, PER),
        tiles(NG, PER),
        pltpu.VMEM(rows, bf),
        pltpu.VMEM((size, width), f32),
        pltpu.VMEM((size, width), f32),
        pltpu.VMEM(rows[:3] + (width,), bf),
        pltpu.VMEM(rows[:3] + (width,), bf),
        tiles(NT_DEV * NG, PER),
        tiles(NT_DEV * NG, PER),
        tiles(NG, PER),
        tiles(2, NG, PER),
        tiles(2, 5, NX),
        tiles(NZ, NG, NX),
        tiles(NX, NZ, NG),
        pltpu.VMEM((CHUNKS, sub, slots, deep // CHUNKS), bf),
        pltpu.VMEM((3 * NG, 8, 128), jnp.int32),
        pltpu.SMEM((3 * NG, 8, 128), jnp.int32),
    ]
    scratch += [dma((CHUNKS,))] * 17 + [dma((CHUNKS // 2,))] * 2 + [dma, dma, dma, dma((5,)), dma]
    query_grad, neighbour_grad = pl.pallas_call(
        kernel,
        out_shape=(
            jax.ShapeDtypeStruct(queries.shape, bf),
            jax.ShapeDtypeStruct(neighbours.shape, bf),
        ),
        in_specs=[sm, sm, vm, vm] + [hbm] * 5,
        out_specs=(hbm, hbm),
        scratch_shapes=scratch,
        name="cross_attention_back",
        compiler_params=pltpu.CompilerParams(
            collective_id=0, has_side_effects=True, vmem_limit_bytes=60 * 2**20
        ),
    )(
        owner_slots, neighbour_owner.T, query_gain.reshape(1, HD), key_gain.reshape(1, HD),
        neighbours, key_weight, value_weight, queries, out_grad,
    )
    return settle(query_grad, neighbour_grad)


def solution(mesh):
    in_specs = (
        P(("seq", "grp"), "tp"),
        P(("seq", "grp"), "tp"),
        P(),
        P(),
        P(None, "tp"),
        P(None, "tp"),
        P(("tp", "grp"), "seq", None),
        P(("seq", "grp"), None),
        P("seq"),
    )
    out_specs = (P(("seq", "grp"), "tp"), P(("tp", "grp"), "seq", None))
    return jax.shard_map(shards, mesh=mesh, in_specs=in_specs, out_specs=out_specs, check_vma=False)
```

```python
import functools
import math

import jax
import jax.numpy as jnp
from jax import lax
from jax.experimental import pallas as pl
from jax.experimental.pallas import tpu as pltpu
from jax.sharding import PartitionSpec as P

HD = 128
CH = 64
EPS = 1e-06
SCALE = 1.0 / math.sqrt(HD)
NT = (((1,), (1,)), ((), ()))
TN = (((0,), (0,)), ((), ()))
NN = (((1,), (0,)), ((), ()))
MESH = pl.DeviceIdType.MESH
NX, NZ, NT_DEV, NG = 4, 8, 4, 2
SUB = 16
PER = 8
CHUNKS = 8


def dot(a, b, dims):
    return lax.dot_general(a, b, dims, preferred_element_type=jnp.float32)


def place():
    s = lax.axis_index("seq")
    return s // NZ, s % NZ, lax.axis_index("tp"), lax.axis_index("grp")


def at(x, z, t, g):
    return (lax.rem(x + NX, NX) * NZ + lax.rem(z + NZ, NZ), lax.rem(t + NT_DEV, NT_DEV), lax.rem(g + NG, NG))


X_PEERS = [(k, 0, 0, 0) for k in (1, 2, 3)]
Z_PEERS = [(0, k, 0, 0) for k in (1, -1, 2, -2, 3, -3)]
Y_PEERS = [(0, 0, t, g) for t in range(NT_DEV) for g in range(NG) if (t, g) != (0, 0)]
META_PEERS = [(0, 1, 0, 1), (0, -1, 0, 1)]


def greet(peers):
    x, z, t, g = place()
    barrier = pltpu.get_barrier_semaphore()
    for dx, dz, dt, dg in peers:
        pl.semaphore_signal(barrier, inc=1, device_id=at(x + dx, z + dz, t + dt, g + dg), device_id_type=MESH)


def met(peers):
    pl.semaphore_wait(pltpu.get_barrier_semaphore(), len(peers))


def push(src, dst, send, recv, device):
    pltpu.make_async_remote_copy(
        src_ref=src, dst_ref=dst, send_sem=send, recv_sem=recv, device_id=device, device_id_type=MESH
    ).start()


def arrive(view, sem):
    pltpu.make_async_copy(view, view, sem).wait()


def choose(tiles, picks, index):
    result = tiles[0]
    for k in range(1, len(tiles)):
        result = jnp.where(index == picks[k], tiles[k], result)
    return result


def attend(done, e_ref, kacc, vacc, wk_ref, wv_ref, q_ref, go_ref, qg_ref, kg_ref, qgrad_ref, dkr_ref, dv_ref):
    rows, width = q_ref.shape
    stretches = rows // CH
    groups, per_dev, sub, enc = e_ref.shape
    keys = groups * 2 * sub
    qgain = qg_ref[...]
    kgain = kg_ref[...]

    def pair(i, carry):
        cols = pl.ds(pl.multiple_of(i * 2 * HD, 2 * HD), 2 * HD)
        last = slice(done, enc)
        enc_rows = e_ref[:, :, :, last].reshape(groups * per_dev * sub, enc - done)
        kr2 = kacc[:, cols] + dot(enc_rows, wk_ref[last, cols], NN)
        val2 = (vacc[:, cols] + dot(enc_rows, wv_ref[last, cols], NN)).astype(jnp.bfloat16)
        for hh in range(2):
            lanes = slice(hh * HD, (hh + 1) * HD)
            head = pl.ds(pl.multiple_of((i * 2 + hh) * HD, HD), HD)
            kr = kr2[:, lanes]
            val = val2[:, lanes].reshape(groups, per_dev, sub, HD)
            kinv = lax.rsqrt(jnp.mean(kr * kr, axis=-1, keepdims=True) + EPS)
            khat = kr * kinv
            kn = (khat * kgain).astype(jnp.bfloat16).reshape(groups, per_dev, sub, HD)
            khat = khat.reshape(groups, per_dev, sub, HD)
            kinv = kinv.reshape(groups, per_dev, sub, 1)
            qx = q_ref[:, head].astype(jnp.float32)
            qinv = lax.rsqrt(jnp.mean(qx * qx, axis=-1, keepdims=True) + EPS)
            qhat = qx * qinv
            qn = (qhat * qgain).astype(jnp.bfloat16)
            go = go_ref[:, head]
            kn_s = [kn[:, 2 * c:2 * c + 2].reshape(keys, HD) for c in range(stretches)]
            val_s = [val[:, 2 * c:2 * c + 2].reshape(keys, HD) for c in range(stretches)]
            toks = [slice(c * CH, (c + 1) * CH) for c in range(stretches)]
            scores = [dot(qn[toks[c]], kn_s[c], NT) for c in range(stretches)]
            dps = [dot(go[toks[c]], val_s[c], NT) for c in range(stretches)]
            half = lax.broadcasted_iota(jnp.int32, (2 * CH, HD), 0) < CH
            zero = jnp.zeros((2 * CH, HD), jnp.bfloat16)
            for j in range(stretches // 2):
                two = slice(j * 2 * CH, (j + 1) * 2 * CH)
                score = jnp.concatenate(scores[2 * j:2 * j + 2], axis=0)
                dp = jnp.concatenate(dps[2 * j:2 * j + 2], axis=0)
                weights = jnp.exp(score * SCALE)
                prob = weights * (1.0 / jnp.sum(weights, axis=-1, keepdims=True))
                inner = jnp.sum(prob * dp, axis=-1, keepdims=True)
                ds = (prob * (dp - inner)).astype(jnp.bfloat16)
                pb = prob.astype(jnp.bfloat16)
                go_2, qn_2 = go[two], qn[two]
                go_b = jnp.concatenate([jnp.where(half, go_2, zero), jnp.where(half, zero, go_2)], axis=1)
                qn_b = jnp.concatenate([jnp.where(half, qn_2, zero), jnp.where(half, zero, qn_2)], axis=1)
                dv2 = dot(pb, go_b, TN).astype(jnp.bfloat16)
                dkn2 = dot(ds, qn_b, TN)
                dqn = jnp.concatenate([dot(ds[k * CH:(k + 1) * CH], kn_s[2 * j + k], NN) for k in range(2)], axis=0)
                qs = dqn * (qgain * SCALE)
                qh = qhat[two]
                qi = jnp.mean(qh * qs, axis=-1, keepdims=True)
                qgrad_ref[two, head] = (qinv[two] * (qs - qh * qi)).astype(jnp.bfloat16)
                for k in range(2):
                    part = slice(2 * (2 * j + k), 2 * (2 * j + k) + 2)
                    ks = dkn2[:, k * HD:(k + 1) * HD] * (kgain * SCALE)
                    kh = khat[:, part].reshape(keys, HD)
                    ki = jnp.mean(kh * ks, axis=-1, keepdims=True)
                    kv = kinv[:, part].reshape(keys, 1)
                    dk = (kv * (ks - kh * ki)).astype(jnp.bfloat16)
                    dkr_ref[:, part, :, head] = dk.reshape(groups, 2, sub, HD)
                    dv_ref[:, part, :, head] = dv2[:, k * HD:(k + 1) * HD].reshape(groups, 2, sub, HD)
        return carry
    lax.fori_loop(0, width // (2 * HD), pair, 0, unroll=2)


def kernel(
    slots_ref, no_ref, qg_ref, kg_ref, nb_hbm, wk_hbm, wv_hbm, q_hbm, go_hbm,
    qgrad_hbm, out_hbm,
    nb, wk, wv, q, go, qgrad, perm, perm_back,
    sent, xr, zb, mg, zr, fin, enc, kacc, vacc, dkr, dv,
    part, yr, gs, r1, fw, rz, fr, placed_ref, meta, mets,
    x_s, x_r, z1_s, z1_r, z2_s, z2_r, y_s, y_r,
    by_s, by_r, r1_s, r1_r, r2_s, r2_r, bx_s, bx_r, out_sem,
    e_s, e_r, m_s, m_r, m_l, in_sem, q_sem,
):
    x, z, t, g = place()
    chunks = CHUNKS
    wide = nb.shape[2] // chunks
    slots = nb.shape[1]
    size = SUB * slots
    peers = X_PEERS + Z_PEERS + Y_PEERS + META_PEERS
    greet(peers)
    loads = [
        pltpu.make_async_copy(src, dst, in_sem.at[k])
        for k, (src, dst) in enumerate(((nb_hbm, nb), (wk_hbm, wk), (wv_hbm, wv), (q_hbm, q), (go_hbm, go)))
    ]
    for load in loads:
        load.start()

    lane8 = lax.broadcasted_iota(jnp.int32, (8, 128), 1)
    row = jnp.zeros((8, 128), jnp.int32)
    for p in range(PER):
        owner = no_ref[p % 2, p // 2]
        row = jnp.where(lane8 == p, owner, row)
        row = jnp.where(lane8 == PER + owner, p, row)
    meta[1 * NG + g] = row

    def block(s):
        number = slots_ref[s]
        return jnp.where(number >= 0, number // PER, -SUB) * SUB

    lane = lax.broadcasted_iota(jnp.int32, (1, 128), 1)
    base = jnp.zeros((1, 128), jnp.int32)
    for s in range(slots):
        base = jnp.where(lax.rem(lane, slots) == s, block(s), base)
    base = base + lane // slots
    order = lax.broadcasted_iota(jnp.int32, (size, 128), 0)
    for k in range(size // 128):
        perm[:, k * 128:(k + 1) * 128] = (order == base + k * (128 // slots)).astype(jnp.bfloat16)
    met(peers)
    mine = meta.at[NG + g]
    push(mine, mine, m_s, m_r, at(x, z, t, g + 1))
    for dg in range(NG):
        push(mine, meta.at[g], m_s, m_r, at(x, z + 1, t, g + dg))
        push(mine, meta.at[2 * NG + g], m_s, m_r, at(x, z - 1, t, g + dg))
    loads[0].wait()

    def columns(c):
        if isinstance(c, int):
            return pl.ds(c * wide, wide)
        return pl.ds(pl.multiple_of(c * wide, wide), wide)

    def stage_x(j):
        cols = pl.ds(pl.multiple_of(j * 2 * wide, 2 * wide), 2 * wide)
        sorted_rows = dot(perm[...], nb[:, :, cols].reshape(size, 2 * wide), NN).astype(jnp.bfloat16)
        for k in range(2):
            c = 2 * j + k
            half = sorted_rows[:, k * wide:(k + 1) * wide]
            sent[c] = half.reshape(NX, NZ, NG, SUB, wide)
            for dx, _, _, _ in X_PEERS:
                to = lax.rem(x + dx, NX)
                push(sent.at[c, to], xr.at[c, NX - dx], x_s.at[c], x_r.at[c], at(to, z, t, g))
            pltpu.make_async_copy(sent.at[c, x], xr.at[c, 0], x_r.at[c]).start()

    def stage_e(j):
        both = pl.ds(2 * j, 2)
        for way, sign in ((0, 1), (1, -1)):
            for k in (3, 2, 1):
                dest = lax.rem(z + sign * (k + 1) + NZ, NZ)
                if k == 3:
                    src, dst = sent.at[both, x, dest, way], zb.at[both, way, 0, 4]
                else:
                    src, dst = sent.at[both, x, dest], zb.at[both, way, 0, pl.ds(2 * (k - 1), 2)]
                push(src, dst, e_s.at[j], e_r.at[j], at(x, z + sign * k, t, g))

    def stage_z1(c):
        arrive(xr.at[c], x_r.at[c])
        others = pl.ds(1, NX - 1)
        for way, sign in ((0, 1), (1, -1)):
            for k in (3, 2, 1):
                dest = lax.rem(z + sign * (k + 1) + NZ, NZ)
                if k == 3:
                    src, dst = xr.at[c, others, dest, way], zb.at[c, way, others, 4]
                else:
                    src, dst = xr.at[c, others, dest], zb.at[c, way, others, pl.ds(2 * (k - 1), 2)]
                push(src, dst, z1_s.at[c], z1_r.at[c], at(x, z + sign * k, t, g))

    def column(owner):
        return lax.rem(owner // NZ - x + NX, NX)

    def stage_z2(c):
        @pl.when(lax.rem(c, 2) == 0)
        def _():
            arrive(zb.at[pl.ds(c, 2), :, 0], e_r.at[c // 2])
        arrive(zb.at[c, :, pl.ds(1, NX - 1)], z1_r.at[c])
        for way, sign in ((0, 1), (1, -1)):
            dest = lax.rem(z + sign + NZ, NZ)
            for h in range(NG):
                far = 3 if h == way else 2
                tiles = [xr[c, k, dest, h] for k in range(NX)]
                for k in range(1, far + 1):
                    part = 4 if k == 3 else 2 * (k - 1) + h
                    tiles += [zb[c, way, j, part] for j in range(NX)]
                for p in range(PER):
                    owner = mets[(1 + sign) * NG + h, 0, p]
                    rel = lax.rem(sign * (z - lax.rem(owner, NZ)) + NZ, NZ)
                    mg[c, way, h, p] = choose(tiles, range(len(tiles)), rel * NX + column(owner))
            push(mg.at[c, way], zr.at[c, way], z2_s.at[c], z2_r.at[c], at(x, z + sign, t, g))

    def stage_y(c):
        arrive(mg.at[c], z2_r.at[c])
        for h in range(NG):
            own = [xr[c, k, z, h] for k in range(NX)]
            for p in range(PER):
                owner = mets[NG + h, 0, p]
                rel = lax.rem(z - lax.rem(owner, NZ) + NZ, NZ)
                back = jnp.where(rel >= (5 if h == 0 else 4), zr[c, 1, h, p], zr[c, 0, h, p])
                near = choose(own, range(NX), column(owner))
                fin[c, h, p] = jnp.where(rel == 0, near, back)
        slot = t * NG + g
        for _, _, dt, dg in Y_PEERS:
            to = lax.rem(g + dg, NG)
            push(fin.at[c, to], enc.at[slot, :, :, columns(c)], y_s.at[c], y_r.at[c], at(x, z, t + dt, to))
        pltpu.make_async_copy(fin.at[c, g], enc.at[slot, :, :, columns(c)], y_r.at[c]).start()

    def project(deep):
        def block_of(k, carry):
            cols = pl.ds(pl.multiple_of(k * 256, 256), 256)
            left = enc[:, :, :, :deep].reshape(size, deep)
            kacc[:, cols] = dot(left, wk[:deep, cols], NN)
            vacc[:, cols] = dot(left, wv[:deep, cols], NN)
            return carry
        lax.fori_loop(0, wk.shape[1] // 256, block_of, 0)

    for j in range(chunks // 2):
        stage_x(j)
        stage_e(j)
    arrive(meta.at[pl.ds(0, 5)], m_r)
    copy = pltpu.make_async_copy(meta, mets, m_l)
    copy.start()
    copy.wait()

    def step(i, carry):
        for lag, stage in ((0, stage_z1), (1, stage_z2), (2, stage_y)):
            @pl.when((i >= lag) & (i < chunks + lag))
            def _(stage=stage, lag=lag):
                stage(i - lag)
        return carry
    lax.fori_loop(0, chunks + 2, step, 0)
    for load in loads[1:]:
        load.wait()
    early = 6
    for c in range(early):
        arrive(enc.at[:, :, :, columns(c)], y_r.at[c])
    project(early * wide)
    for c in range(early, chunks):
        arrive(enc.at[:, :, :, columns(c)], y_r.at[c])

    attend(early * wide, enc, kacc, vacc, wk, wv, q, go, qg_ref, kg_ref, qgrad, dkr, dv)
    give = pltpu.make_async_copy(qgrad, qgrad_hbm, q_sem)
    give.start()

    def back_y(c):
        slot = t * NG + g
        rows = columns(c)
        total = dot(dkr[...].reshape(size, -1), wk[rows, :], NT)
        total = total + dot(dv[...].reshape(size, -1), wv[rows, :], NT)
        part[c] = total.astype(jnp.bfloat16).reshape(NT_DEV * NG, PER, SUB, wide)
        for _, _, dt, dg in Y_PEERS:
            tt, gg = lax.rem(t + dt, NT_DEV), lax.rem(g + dg, NG)
            push(part.at[c, tt * NG + gg], yr.at[c, slot], by_s.at[c], by_r.at[c], at(x, z, tt, gg))
        pltpu.make_async_copy(part.at[c, slot], yr.at[c, slot], by_r.at[c]).start()

    def back_r1(c):
        arrive(yr.at[c], by_r.at[c])
        for h in range(NG):
            total = yr[c, h].astype(jnp.float32)
            for k in range(1, NT_DEV):
                total = total + yr[c, k * NG + h].astype(jnp.float32)
            gs[c, h] = total.astype(jnp.bfloat16)
        push(gs.at[c], r1.at[c, 0], r1_s.at[c], r1_r.at[c], at(x, z + 1, t, g))
        push(gs.at[c], r1.at[c, 1], r1_s.at[c], r1_r.at[c], at(x, z - 1, t, g))

    def select(tiles, near, h, row, xo):
        position = mets[near * NG + h, 0, PER + xo * NZ + row]
        return choose(tiles, range(PER), position)

    def back_r2(c):
        arrive(r1.at[c], r1_r.at[c])
        for way, sign in ((0, 1), (1, -1)):
            near = 0 if way == 0 else 2
            block = lax.rem(z - sign + NZ, NZ)
            for h in range(NG):
                far = 3 if h == way else 2
                tiles = [r1[c, way, h, p] for p in range(PER)]
                for k in range(far + 1):
                    row = lax.rem(z + sign * k + NZ, NZ)
                    part = 4 if k == 3 else 2 * (k - 1) + h
                    for xo in range(NX):
                        value = select(tiles, near, h, row, xo)
                        if k == 0:
                            rz[c, block, h, xo] = value
                        else:
                            fw[c, way, part, xo] = value
            for k in (3, 2, 1):
                if k == 3:
                    src, dst = fw.at[c, way, 4], rz.at[c, block, way]
                else:
                    src, dst = fw.at[c, way, pl.ds(2 * (k - 1), 2)], rz.at[c, block]
                push(src, dst, r2_s.at[c], r2_r.at[c], at(x, z + sign * k, t, g))
        for h in range(NG):
            tiles = [gs[c, h, p] for p in range(PER)]
            for xo in range(NX):
                rz[c, z, h, xo] = select(tiles, 1, h, z, xo)

    def back_x(c):
        arrive(fw.at[c], r2_r.at[c])
        for dx, _, _, _ in X_PEERS:
            to = lax.rem(x + dx, NX)
            push(rz.at[c, :, :, to], fr.at[c, x], bx_s.at[c], bx_r.at[c], at(to, z, t, g))
        pltpu.make_async_copy(rz.at[c, :, :, x], fr.at[c, x], bx_r.at[c]).start()

    def back_out(c):
        arrive(fr.at[c], bx_r.at[c])
        rows = fr[c].reshape(size, wide)
        placed = dot(perm_back[...], rows, NN).astype(jnp.bfloat16)
        placed_ref[c] = placed.reshape(SUB, slots, wide)
        pltpu.make_async_copy(placed_ref.at[c], out_hbm.at[:, :, columns(c)], out_sem.at[c]).start()

    def back_step(i, carry):
        for lag, stage in ((4, back_r2), (2, back_r1), (0, back_y), (5, back_x), (6, back_out)):
            @pl.when((i >= lag) & (i < chunks + lag))
            def _(stage=stage, lag=lag):
                stage(i - lag)

        @pl.when(i == 0)
        def _():
            order = lax.broadcasted_iota(jnp.int32, (size, 128), 1)
            down = lax.broadcasted_iota(jnp.int32, (8, 128), 0)
            parts = []
            for k in range(slots // 8):
                value = jnp.zeros((8, 128), jnp.int32)
                for s in range(8):
                    value = jnp.where(down == s, block(k * 8 + s), value)
                parts.append(value)
            rows = jnp.concatenate(parts, axis=0)
            rows = jnp.concatenate([rows + r for r in range(SUB)], axis=0)
            for k in range(size // 128):
                perm_back[:, k * 128:(k + 1) * 128] = (order + k * 128 == rows).astype(jnp.bfloat16)
        return carry
    lax.fori_loop(0, chunks + 6, back_step, 0)

    def drain(c, carry):
        arrive(sent.at[c, pl.ds(0, 3)], x_s.at[c])
        arrive(zb.at[c, :, pl.ds(1, NX - 1)], z1_s.at[c])
        arrive(mg.at[c], z2_s.at[c])
        arrive(part.at[c, pl.ds(0, 7)], y_s.at[c])
        arrive(part.at[c, pl.ds(0, 7)], by_s.at[c])
        arrive(r1.at[c], r1_s.at[c])
        arrive(fw.at[c], r2_s.at[c])
        arrive(fr.at[c, pl.ds(0, 3)], bx_s.at[c])
        pltpu.make_async_copy(placed_ref.at[c], out_hbm.at[:, :, columns(c)], out_sem.at[c]).wait()
        return carry
    lax.fori_loop(0, chunks, drain, 0)
    for j in range(chunks // 2):
        arrive(zb.at[pl.ds(2 * j, 2), :, 0], e_s.at[j])
    arrive(meta.at[pl.ds(0, 5)], m_s)
    give.wait()


def settle_kernel(a_ref, b_ref, x_ref, y_ref):
    x_ref[...] = a_ref[...]
    y_ref[...] = b_ref[...]


def settle(a, b):
    steps = 2
    a_spec = pl.BlockSpec((a.shape[0] // steps, a.shape[1]), lambda i: (i, 0))
    b_spec = pl.BlockSpec((b.shape[0] // steps,) + b.shape[1:], lambda i: (i, 0, 0))
    return pl.pallas_call(
        settle_kernel,
        grid=(steps,),
        out_shape=(jax.ShapeDtypeStruct(a.shape, a.dtype), jax.ShapeDtypeStruct(b.shape, b.dtype)),
        in_specs=[a_spec, b_spec],
        out_specs=(a_spec, b_spec),
        name="settle",
    )(a, b)


def shards(
    queries,
    out_grad,
    query_gain,
    key_gain,
    key_weight,
    value_weight,
    neighbours,
    neighbour_owner,
    owner_slots,
):
    tokens, width = queries.shape
    sub, slots, deep = neighbours.shape
    bf = jnp.bfloat16
    f32 = jnp.float32
    size = sub * slots
    end = (SUB, deep // CHUNKS)
    rows = (NT_DEV * NG, PER, SUB, deep)
    vm = pl.BlockSpec(memory_space=pltpu.VMEM)
    sm = pl.BlockSpec(memory_space=pltpu.SMEM)
    hbm = pl.BlockSpec(memory_space=pl.ANY)
    dma = pltpu.SemaphoreType.DMA

    def tiles(*lead):
        return pltpu.VMEM((CHUNKS,) + lead + end, bf)
    scratch = [
        pltpu.VMEM(neighbours.shape, bf),
        pltpu.VMEM(key_weight.shape, bf),
        pltpu.VMEM(value_weight.shape, bf),
        pltpu.VMEM(queries.shape, bf),
        pltpu.VMEM(out_grad.shape, bf),
        pltpu.VMEM(queries.shape, bf),
        pltpu.VMEM((size, size), bf),
        pltpu.VMEM((size, size), bf),
        tiles(NX, NZ, NG),
        tiles(NX, NZ, NG),
        tiles(2, NX, 5),
        tiles(2, NG, PER),
        tiles(2, NG, PER),
        tiles(NG, PER),
        pltpu.VMEM(rows, bf),
        pltpu.VMEM((size, width), f32),
        pltpu.VMEM((size, width), f32),
        pltpu.VMEM(rows[:3] + (width,), bf),
        pltpu.VMEM(rows[:3] + (width,), bf),
        tiles(NT_DEV * NG, PER),
        tiles(NT_DEV * NG, PER),
        tiles(NG, PER),
        tiles(2, NG, PER),
        tiles(2, 5, NX),
        tiles(NZ, NG, NX),
        tiles(NX, NZ, NG),
        pltpu.VMEM((CHUNKS, sub, slots, deep // CHUNKS), bf),
        pltpu.VMEM((3 * NG, 8, 128), jnp.int32),
        pltpu.SMEM((3 * NG, 8, 128), jnp.int32),
    ]
    scratch += [dma((CHUNKS,))] * 17 + [dma((CHUNKS // 2,))] * 2 + [dma, dma, dma, dma((5,)), dma]
    query_grad, neighbour_grad = pl.pallas_call(
        kernel,
        out_shape=(
            jax.ShapeDtypeStruct(queries.shape, bf),
            jax.ShapeDtypeStruct(neighbours.shape, bf),
        ),
        in_specs=[sm, sm, vm, vm] + [hbm] * 5,
        out_specs=(hbm, hbm),
        scratch_shapes=scratch,
        name="cross_attention_back",
        compiler_params=pltpu.CompilerParams(
            collective_id=0, has_side_effects=True, vmem_limit_bytes=60 * 2**20
        ),
    )(
        owner_slots, neighbour_owner.T, query_gain.reshape(1, HD), key_gain.reshape(1, HD),
        neighbours, key_weight, value_weight, queries, out_grad,
    )
    return settle(query_grad, neighbour_grad)


def solution(mesh):
    in_specs = (
        P(("seq", "grp"), "tp"),
        P(("seq", "grp"), "tp"),
        P(),
        P(),
        P(None, "tp"),
        P(None, "tp"),
        P(("tp", "grp"), "seq", None),
        P(("seq", "grp"), None),
        P("seq"),
    )
    out_specs = (P(("seq", "grp"), "tp"), P(("tp", "grp"), "seq", None))
    return jax.shard_map(shards, mesh=mesh, in_specs=in_specs, out_specs=out_specs, check_vma=False)
```

```python
import functools
import math

import jax
import jax.numpy as jnp
from jax import lax
from jax.experimental import pallas as pl
from jax.experimental.pallas import tpu as pltpu
from jax.sharding import PartitionSpec as P

HD = 128
CH = 64
EPS = 1e-06
SCALE = 1.0 / math.sqrt(HD)
NT = (((1,), (1,)), ((), ()))
TN = (((0,), (0,)), ((), ()))
NN = (((1,), (0,)), ((), ()))
MESH = pl.DeviceIdType.MESH
NX, NZ, NT_DEV, NG = 4, 8, 4, 2
SUB = 16
PER = 8
CHUNKS = 8


def dot(a, b, dims):
    return lax.dot_general(a, b, dims, preferred_element_type=jnp.float32)


def place():
    s = lax.axis_index("seq")
    return s // NZ, s % NZ, lax.axis_index("tp"), lax.axis_index("grp")


def at(x, z, t, g):
    return (lax.rem(x + NX, NX) * NZ + lax.rem(z + NZ, NZ), lax.rem(t + NT_DEV, NT_DEV), lax.rem(g + NG, NG))


X_PEERS = [(k, 0, 0, 0) for k in (1, 2, 3)]
Z_PEERS = [(0, k, 0, 0) for k in (1, -1, 2, -2, 3, -3)]
Y_PEERS = [(0, 0, t, g) for t in range(NT_DEV) for g in range(NG) if (t, g) != (0, 0)]
META_PEERS = [(0, 1, 0, 1), (0, -1, 0, 1)]


def greet(peers):
    x, z, t, g = place()
    barrier = pltpu.get_barrier_semaphore()
    for dx, dz, dt, dg in peers:
        pl.semaphore_signal(barrier, inc=1, device_id=at(x + dx, z + dz, t + dt, g + dg), device_id_type=MESH)


def met(peers):
    pl.semaphore_wait(pltpu.get_barrier_semaphore(), len(peers))


def push(src, dst, send, recv, device):
    pltpu.make_async_remote_copy(
        src_ref=src, dst_ref=dst, send_sem=send, recv_sem=recv, device_id=device, device_id_type=MESH
    ).start()


def arrive(view, sem):
    pltpu.make_async_copy(view, view, sem).wait()


def choose(tiles, picks, index):
    result = tiles[0]
    for k in range(1, len(tiles)):
        result = jnp.where(index == picks[k], tiles[k], result)
    return result


def attend(done, e_ref, kacc, vacc, wk_ref, wv_ref, q_ref, go_ref, qg_ref, kg_ref, qgrad_ref, dkr_ref, dv_ref):
    rows, width = q_ref.shape
    stretches = rows // CH
    groups, per_dev, sub, enc = e_ref.shape
    keys = groups * 2 * sub
    qgain = qg_ref[...]
    kgain = kg_ref[...]

    def pair(i, carry):
        cols = pl.ds(pl.multiple_of(i * 2 * HD, 2 * HD), 2 * HD)
        last = slice(done, enc)
        enc_rows = e_ref[:, :, :, last].reshape(groups * per_dev * sub, enc - done)
        kr2 = kacc[:, cols] + dot(enc_rows, wk_ref[last, cols], NN)
        val2 = (vacc[:, cols] + dot(enc_rows, wv_ref[last, cols], NN)).astype(jnp.bfloat16)
        for hh in range(2):
            lanes = slice(hh * HD, (hh + 1) * HD)
            head = pl.ds(pl.multiple_of((i * 2 + hh) * HD, HD), HD)
            kr = kr2[:, lanes]
            val = val2[:, lanes].reshape(groups, per_dev, sub, HD)
            kinv = lax.rsqrt(jnp.mean(kr * kr, axis=-1, keepdims=True) + EPS)
            khat = kr * kinv
            kn = (khat * kgain).astype(jnp.bfloat16).reshape(groups, per_dev, sub, HD)
            khat = khat.reshape(groups, per_dev, sub, HD)
            kinv = kinv.reshape(groups, per_dev, sub, 1)
            qx = q_ref[:, head].astype(jnp.float32)
            qinv = lax.rsqrt(jnp.mean(qx * qx, axis=-1, keepdims=True) + EPS)
            qhat = qx * qinv
            qn = (qhat * qgain).astype(jnp.bfloat16)
            go = go_ref[:, head]
            kn_s = [kn[:, 2 * c:2 * c + 2].reshape(keys, HD) for c in range(stretches)]
            val_s = [val[:, 2 * c:2 * c + 2].reshape(keys, HD) for c in range(stretches)]
            toks = [slice(c * CH, (c + 1) * CH) for c in range(stretches)]
            scores = [dot(qn[toks[c]], kn_s[c], NT) for c in range(stretches)]
            dps = [dot(go[toks[c]], val_s[c], NT) for c in range(stretches)]
            half = lax.broadcasted_iota(jnp.int32, (2 * CH, HD), 0) < CH
            zero = jnp.zeros((2 * CH, HD), jnp.bfloat16)
            for j in range(stretches // 2):
                two = slice(j * 2 * CH, (j + 1) * 2 * CH)
                score = jnp.concatenate(scores[2 * j:2 * j + 2], axis=0)
                dp = jnp.concatenate(dps[2 * j:2 * j + 2], axis=0)
                weights = jnp.exp(score * SCALE)
                prob = weights * (1.0 / jnp.sum(weights, axis=-1, keepdims=True))
                inner = jnp.sum(prob * dp, axis=-1, keepdims=True)
                ds = (prob * (dp - inner)).astype(jnp.bfloat16)
                pb = prob.astype(jnp.bfloat16)
                go_2, qn_2 = go[two], qn[two]
                go_b = jnp.concatenate([jnp.where(half, go_2, zero), jnp.where(half, zero, go_2)], axis=1)
                qn_b = jnp.concatenate([jnp.where(half, qn_2, zero), jnp.where(half, zero, qn_2)], axis=1)
                dv2 = dot(pb, go_b, TN).astype(jnp.bfloat16)
                dkn2 = dot(ds, qn_b, TN)
                dqn = jnp.concatenate([dot(ds[k * CH:(k + 1) * CH], kn_s[2 * j + k], NN) for k in range(2)], axis=0)
                qs = dqn * (qgain * SCALE)
                qh = qhat[two]
                qi = jnp.mean(qh * qs, axis=-1, keepdims=True)
                qgrad_ref[two, head] = (qinv[two] * (qs - qh * qi)).astype(jnp.bfloat16)
                for k in range(2):
                    part = slice(2 * (2 * j + k), 2 * (2 * j + k) + 2)
                    ks = dkn2[:, k * HD:(k + 1) * HD] * (kgain * SCALE)
                    kh = khat[:, part].reshape(keys, HD)
                    ki = jnp.mean(kh * ks, axis=-1, keepdims=True)
                    kv = kinv[:, part].reshape(keys, 1)
                    dk = (kv * (ks - kh * ki)).astype(jnp.bfloat16)
                    dkr_ref[:, part, :, head] = dk.reshape(groups, 2, sub, HD)
                    dv_ref[:, part, :, head] = dv2[:, k * HD:(k + 1) * HD].reshape(groups, 2, sub, HD)
        return carry
    lax.fori_loop(0, width // (2 * HD), pair, 0, unroll=2)


def kernel(
    slots_ref, no_ref, qg_ref, kg_ref, nb_hbm, wk_hbm, wv_hbm, q_hbm, go_hbm,
    qgrad_hbm, out_hbm,
    nb, wk, wv, q, go, qgrad, perm, perm_back,
    sent, xr, zb, mg, zr, fin, enc, kacc, vacc, dkr, dv,
    part, yr, gs, r1, fw, rz, fr, placed_ref, meta, mets,
    x_s, x_r, z1_s, z1_r, z2_s, z2_r, y_s, y_r,
    by_s, by_r, r1_s, r1_r, r2_s, r2_r, bx_s, bx_r, out_sem,
    e_s, e_r, m_s, m_r, m_l, in_sem, q_sem,
):
    x, z, t, g = place()
    chunks = CHUNKS
    wide = nb.shape[2] // chunks
    slots = nb.shape[1]
    size = SUB * slots
    peers = X_PEERS + Z_PEERS + Y_PEERS + META_PEERS
    greet(peers)
    loads = [
        pltpu.make_async_copy(src, dst, in_sem.at[k])
        for k, (src, dst) in enumerate(((nb_hbm, nb), (wk_hbm, wk), (wv_hbm, wv), (q_hbm, q), (go_hbm, go)))
    ]
    for load in loads:
        load.start()

    lane8 = lax.broadcasted_iota(jnp.int32, (8, 128), 1)
    row = jnp.zeros((8, 128), jnp.int32)
    for p in range(PER):
        owner = no_ref[p % 2, p // 2]
        row = jnp.where(lane8 == p, owner, row)
        row = jnp.where(lane8 == PER + owner, p, row)
    meta[1 * NG + g] = row

    def block(s):
        number = slots_ref[s]
        return jnp.where(number >= 0, number // PER, -SUB) * SUB

    lane = lax.broadcasted_iota(jnp.int32, (1, 128), 1)
    base = jnp.zeros((1, 128), jnp.int32)
    for s in range(slots):
        base = jnp.where(lax.rem(lane, slots) == s, block(s), base)
    base = base + lane // slots
    order = lax.broadcasted_iota(jnp.int32, (size, 128), 0)
    for k in range(size // 128):
        perm[:, k * 128:(k + 1) * 128] = (order == base + k * (128 // slots)).astype(jnp.bfloat16)
    met(peers)
    mine = meta.at[NG + g]
    push(mine, mine, m_s, m_r, at(x, z, t, g + 1))
    for dg in range(NG):
        push(mine, meta.at[g], m_s, m_r, at(x, z + 1, t, g + dg))
        push(mine, meta.at[2 * NG + g], m_s, m_r, at(x, z - 1, t, g + dg))
    loads[0].wait()

    def columns(c):
        if isinstance(c, int):
            return pl.ds(c * wide, wide)
        return pl.ds(pl.multiple_of(c * wide, wide), wide)

    def stage_x(j):
        cols = pl.ds(pl.multiple_of(j * 2 * wide, 2 * wide), 2 * wide)
        sorted_rows = dot(perm[...], nb[:, :, cols].reshape(size, 2 * wide), NN).astype(jnp.bfloat16)
        for k in range(2):
            c = 2 * j + k
            half = sorted_rows[:, k * wide:(k + 1) * wide]
            sent[c] = half.reshape(NX, NZ, NG, SUB, wide)
            for dx, _, _, _ in X_PEERS:
                to = lax.rem(x + dx, NX)
                push(sent.at[c, to], xr.at[c, NX - dx], x_s.at[c], x_r.at[c], at(to, z, t, g))
            pltpu.make_async_copy(sent.at[c, x], xr.at[c, 0], x_r.at[c]).start()

    def stage_e(j):
        both = pl.ds(2 * j, 2)
        for way, sign in ((0, 1), (1, -1)):
            for k in (3, 2, 1):
                dest = lax.rem(z + sign * (k + 1) + NZ, NZ)
                if k == 3:
                    src, dst = sent.at[both, x, dest, way], zb.at[both, way, 0, 4]
                else:
                    src, dst = sent.at[both, x, dest], zb.at[both, way, 0, pl.ds(2 * (k - 1), 2)]
                push(src, dst, e_s.at[j], e_r.at[j], at(x, z + sign * k, t, g))

    def stage_z1(c):
        arrive(xr.at[c], x_r.at[c])
        others = pl.ds(1, NX - 1)
        for way, sign in ((0, 1), (1, -1)):
            for k in (3, 2, 1):
                dest = lax.rem(z + sign * (k + 1) + NZ, NZ)
                if k == 3:
                    src, dst = xr.at[c, others, dest, way], zb.at[c, way, others, 4]
                else:
                    src, dst = xr.at[c, others, dest], zb.at[c, way, others, pl.ds(2 * (k - 1), 2)]
                push(src, dst, z1_s.at[c], z1_r.at[c], at(x, z + sign * k, t, g))

    def column(owner):
        return lax.rem(owner // NZ - x + NX, NX)

    def stage_z2(c):
        @pl.when(lax.rem(c, 2) == 0)
        def _():
            arrive(zb.at[pl.ds(c, 2), :, 0], e_r.at[c // 2])
        arrive(zb.at[c, :, pl.ds(1, NX - 1)], z1_r.at[c])
        for way, sign in ((0, 1), (1, -1)):
            dest = lax.rem(z + sign + NZ, NZ)
            for h in range(NG):
                far = 3 if h == way else 2
                tiles = [xr[c, k, dest, h] for k in range(NX)]
                for k in range(1, far + 1):
                    part = 4 if k == 3 else 2 * (k - 1) + h
                    tiles += [zb[c, way, j, part] for j in range(NX)]
                for p in range(PER):
                    owner = mets[(1 + sign) * NG + h, 0, p]
                    rel = lax.rem(sign * (z - lax.rem(owner, NZ)) + NZ, NZ)
                    mg[c, way, h, p] = choose(tiles, range(len(tiles)), rel * NX + column(owner))
            push(mg.at[c, way], zr.at[c, way], z2_s.at[c], z2_r.at[c], at(x, z + sign, t, g))

    def stage_y(c):
        arrive(mg.at[c], z2_r.at[c])
        for h in range(NG):
            own = [xr[c, k, z, h] for k in range(NX)]
            for p in range(PER):
                owner = mets[NG + h, 0, p]
                rel = lax.rem(z - lax.rem(owner, NZ) + NZ, NZ)
                back = jnp.where(rel >= (5 if h == 0 else 4), zr[c, 1, h, p], zr[c, 0, h, p])
                near = choose(own, range(NX), column(owner))
                fin[c, h, p] = jnp.where(rel == 0, near, back)
        slot = t * NG + g
        for _, _, dt, dg in Y_PEERS:
            to = lax.rem(g + dg, NG)
            push(fin.at[c, to], enc.at[slot, :, :, columns(c)], y_s.at[c], y_r.at[c], at(x, z, t + dt, to))
        pltpu.make_async_copy(fin.at[c, g], enc.at[slot, :, :, columns(c)], y_r.at[c]).start()

    def project(deep):
        def block_of(k, carry):
            cols = pl.ds(pl.multiple_of(k * 256, 256), 256)
            left = enc[:, :, :, :deep].reshape(size, deep)
            kacc[:, cols] = dot(left, wk[:deep, cols], NN)
            vacc[:, cols] = dot(left, wv[:deep, cols], NN)
            return carry
        lax.fori_loop(0, wk.shape[1] // 256, block_of, 0)

    for j in range(chunks // 2):
        stage_x(j)
        stage_e(j)
    across = lax.broadcasted_iota(jnp.int32, (size, 128), 1)
    down = lax.broadcasted_iota(jnp.int32, (8, 128), 0)
    parts = []
    for k in range(slots // 8):
        value = jnp.zeros((8, 128), jnp.int32)
        for s in range(8):
            value = jnp.where(down == s, block(k * 8 + s), value)
        parts.append(value)
    rows = jnp.concatenate(parts, axis=0)
    rows = jnp.concatenate([rows + r for r in range(SUB)], axis=0)
    for k in range(size // 128):
        perm_back[:, k * 128:(k + 1) * 128] = (across + k * 128 == rows).astype(jnp.bfloat16)
    arrive(meta.at[pl.ds(0, 5)], m_r)
    copy = pltpu.make_async_copy(meta, mets, m_l)
    copy.start()
    copy.wait()

    def step(i, carry):
        for lag, stage in ((0, stage_z1), (1, stage_z2), (2, stage_y)):
            @pl.when((i >= lag) & (i < chunks + lag))
            def _(stage=stage, lag=lag):
                stage(i - lag)
        return carry
    lax.fori_loop(0, chunks + 2, step, 0)
    for load in loads[1:]:
        load.wait()
    early = 6
    for c in range(early):
        arrive(enc.at[:, :, :, columns(c)], y_r.at[c])
    project(early * wide)
    for c in range(early, chunks):
        arrive(enc.at[:, :, :, columns(c)], y_r.at[c])

    attend(early * wide, enc, kacc, vacc, wk, wv, q, go, qg_ref, kg_ref, qgrad, dkr, dv)
    give = pltpu.make_async_copy(qgrad, qgrad_hbm, q_sem)
    give.start()

    def back_y(c):
        slot = t * NG + g
        rows = columns(c)
        total = dot(dkr[...].reshape(size, -1), wk[rows, :], NT)
        total = total + dot(dv[...].reshape(size, -1), wv[rows, :], NT)
        part[c] = total.astype(jnp.bfloat16).reshape(NT_DEV * NG, PER, SUB, wide)
        for _, _, dt, dg in Y_PEERS:
            tt, gg = lax.rem(t + dt, NT_DEV), lax.rem(g + dg, NG)
            push(part.at[c, tt * NG + gg], yr.at[c, slot], by_s.at[c], by_r.at[c], at(x, z, tt, gg))
        pltpu.make_async_copy(part.at[c, slot], yr.at[c, slot], by_r.at[c]).start()

    def back_r1(c):
        arrive(yr.at[c], by_r.at[c])
        for h in range(NG):
            total = yr[c, h].astype(jnp.float32)
            for k in range(1, NT_DEV):
                total = total + yr[c, k * NG + h].astype(jnp.float32)
            gs[c, h] = total.astype(jnp.bfloat16)
        push(gs.at[c], r1.at[c, 0], r1_s.at[c], r1_r.at[c], at(x, z + 1, t, g))
        push(gs.at[c], r1.at[c, 1], r1_s.at[c], r1_r.at[c], at(x, z - 1, t, g))

    def select(tiles, near, h, row, xo):
        position = mets[near * NG + h, 0, PER + xo * NZ + row]
        return choose(tiles, range(PER), position)

    def back_r2(c):
        arrive(r1.at[c], r1_r.at[c])
        for way, sign in ((0, 1), (1, -1)):
            near = 0 if way == 0 else 2
            block = lax.rem(z - sign + NZ, NZ)
            for h in range(NG):
                far = 3 if h == way else 2
                tiles = [r1[c, way, h, p] for p in range(PER)]
                for k in range(far + 1):
                    row = lax.rem(z + sign * k + NZ, NZ)
                    part = 4 if k == 3 else 2 * (k - 1) + h
                    for xo in range(NX):
                        value = select(tiles, near, h, row, xo)
                        if k == 0:
                            rz[c, block, h, xo] = value
                        else:
                            fw[c, way, part, xo] = value
            for k in (3, 2, 1):
                if k == 3:
                    src, dst = fw.at[c, way, 4], rz.at[c, block, way]
                else:
                    src, dst = fw.at[c, way, pl.ds(2 * (k - 1), 2)], rz.at[c, block]
                push(src, dst, r2_s.at[c], r2_r.at[c], at(x, z + sign * k, t, g))
        for h in range(NG):
            tiles = [gs[c, h, p] for p in range(PER)]
            for xo in range(NX):
                rz[c, z, h, xo] = select(tiles, 1, h, z, xo)

    def back_x(c):
        arrive(fw.at[c], r2_r.at[c])
        for dx, _, _, _ in X_PEERS:
            to = lax.rem(x + dx, NX)
            push(rz.at[c, :, :, to], fr.at[c, x], bx_s.at[c], bx_r.at[c], at(to, z, t, g))
        pltpu.make_async_copy(rz.at[c, :, :, x], fr.at[c, x], bx_r.at[c]).start()

    def back_out(c):
        arrive(fr.at[c], bx_r.at[c])
        rows = fr[c].reshape(size, wide)
        placed = dot(perm_back[...], rows, NN).astype(jnp.bfloat16)
        placed_ref[c] = placed.reshape(SUB, slots, wide)
        pltpu.make_async_copy(placed_ref.at[c], out_hbm.at[:, :, columns(c)], out_sem.at[c]).start()

    def back_step(i, carry):
        for lag, stage in ((4, back_r2), (2, back_r1), (0, back_y), (5, back_x), (6, back_out)):
            @pl.when((i >= lag) & (i < chunks + lag))
            def _(stage=stage, lag=lag):
                stage(i - lag)

        return carry
    lax.fori_loop(0, chunks + 6, back_step, 0)

    def drain(c, carry):
        arrive(sent.at[c, pl.ds(0, 3)], x_s.at[c])
        arrive(zb.at[c, :, pl.ds(1, NX - 1)], z1_s.at[c])
        arrive(mg.at[c], z2_s.at[c])
        arrive(part.at[c, pl.ds(0, 7)], y_s.at[c])
        arrive(part.at[c, pl.ds(0, 7)], by_s.at[c])
        arrive(r1.at[c], r1_s.at[c])
        arrive(fw.at[c], r2_s.at[c])
        arrive(fr.at[c, pl.ds(0, 3)], bx_s.at[c])
        pltpu.make_async_copy(placed_ref.at[c], out_hbm.at[:, :, columns(c)], out_sem.at[c]).wait()
        return carry
    lax.fori_loop(0, chunks, drain, 0)
    for j in range(chunks // 2):
        arrive(zb.at[pl.ds(2 * j, 2), :, 0], e_s.at[j])
    arrive(meta.at[pl.ds(0, 5)], m_s)
    give.wait()


def settle_kernel(a_ref, b_ref, x_ref, y_ref, a_held, b_held, in_sem, out_sem):
    moves = []
    for src, held, dst, pieces in ((b_ref, b_held, y_ref, 8), (a_ref, a_held, x_ref, 2)):
        rows = src.shape[0] // pieces
        for k in range(pieces):
            part = pl.ds(k * rows, rows)
            n = len(moves)
            moves.append((
                pltpu.make_async_copy(src.at[part], held.at[part], in_sem.at[n]),
                pltpu.make_async_copy(held.at[part], dst.at[part], out_sem.at[n]),
            ))
    for load, _ in moves:
        load.start()
    for load, store in moves:
        load.wait()
        store.start()
    for _, store in moves:
        store.wait()


def settle(a, b):
    hbm = pl.BlockSpec(memory_space=pl.ANY)
    return pl.pallas_call(
        settle_kernel,
        out_shape=(jax.ShapeDtypeStruct(a.shape, a.dtype), jax.ShapeDtypeStruct(b.shape, b.dtype)),
        in_specs=[hbm, hbm],
        out_specs=(hbm, hbm),
        scratch_shapes=[
            pltpu.VMEM(a.shape, a.dtype),
            pltpu.VMEM(b.shape, b.dtype),
            pltpu.SemaphoreType.DMA((10,)),
            pltpu.SemaphoreType.DMA((10,)),
        ],
        name="settle",
        compiler_params=pltpu.CompilerParams(vmem_limit_bytes=60 * 2**20),
    )(a, b)


def shards(
    queries,
    out_grad,
    query_gain,
    key_gain,
    key_weight,
    value_weight,
    neighbours,
    neighbour_owner,
    owner_slots,
):
    tokens, width = queries.shape
    sub, slots, deep = neighbours.shape
    bf = jnp.bfloat16
    f32 = jnp.float32
    size = sub * slots
    end = (SUB, deep // CHUNKS)
    rows = (NT_DEV * NG, PER, SUB, deep)
    vm = pl.BlockSpec(memory_space=pltpu.VMEM)
    sm = pl.BlockSpec(memory_space=pltpu.SMEM)
    hbm = pl.BlockSpec(memory_space=pl.ANY)
    dma = pltpu.SemaphoreType.DMA

    def tiles(*lead):
        return pltpu.VMEM((CHUNKS,) + lead + end, bf)
    scratch = [
        pltpu.VMEM(neighbours.shape, bf),
        pltpu.VMEM(key_weight.shape, bf),
        pltpu.VMEM(value_weight.shape, bf),
        pltpu.VMEM(queries.shape, bf),
        pltpu.VMEM(out_grad.shape, bf),
        pltpu.VMEM(queries.shape, bf),
        pltpu.VMEM((size, size), bf),
        pltpu.VMEM((size, size), bf),
        tiles(NX, NZ, NG),
        tiles(NX, NZ, NG),
        tiles(2, NX, 5),
        tiles(2, NG, PER),
        tiles(2, NG, PER),
        tiles(NG, PER),
        pltpu.VMEM(rows, bf),
        pltpu.VMEM((size, width), f32),
        pltpu.VMEM((size, width), f32),
        pltpu.VMEM(rows[:3] + (width,), bf),
        pltpu.VMEM(rows[:3] + (width,), bf),
        tiles(NT_DEV * NG, PER),
        tiles(NT_DEV * NG, PER),
        tiles(NG, PER),
        tiles(2, NG, PER),
        tiles(2, 5, NX),
        tiles(NZ, NG, NX),
        tiles(NX, NZ, NG),
        pltpu.VMEM((CHUNKS, sub, slots, deep // CHUNKS), bf),
        pltpu.VMEM((3 * NG, 8, 128), jnp.int32),
        pltpu.SMEM((3 * NG, 8, 128), jnp.int32),
    ]
    scratch += [dma((CHUNKS,))] * 17 + [dma((CHUNKS // 2,))] * 2 + [dma, dma, dma, dma((5,)), dma]
    query_grad, neighbour_grad = pl.pallas_call(
        kernel,
        out_shape=(
            jax.ShapeDtypeStruct(queries.shape, bf),
            jax.ShapeDtypeStruct(neighbours.shape, bf),
        ),
        in_specs=[sm, sm, vm, vm] + [hbm] * 5,
        out_specs=(hbm, hbm),
        scratch_shapes=scratch,
        name="cross_attention_back",
        compiler_params=pltpu.CompilerParams(
            collective_id=0, has_side_effects=True, vmem_limit_bytes=60 * 2**20
        ),
    )(
        owner_slots, neighbour_owner.T, query_gain.reshape(1, HD), key_gain.reshape(1, HD),
        neighbours, key_weight, value_weight, queries, out_grad,
    )
    return settle(query_grad, neighbour_grad)


def solution(mesh):
    in_specs = (
        P(("seq", "grp"), "tp"),
        P(("seq", "grp"), "tp"),
        P(),
        P(),
        P(None, "tp"),
        P(None, "tp"),
        P(("tp", "grp"), "seq", None),
        P(("seq", "grp"), None),
        P("seq"),
    )
    out_specs = (P(("seq", "grp"), "tp"), P(("tp", "grp"), "seq", None))
    return jax.shard_map(shards, mesh=mesh, in_specs=in_specs, out_specs=out_specs, check_vma=False)
```
